32 devices in a mesh: groups: 2 (over y), row: 4 (over z), col: 2 (over x), layer: 2 (over core).
Axes of the slice: x: 2, y: 2, z: 4, core: 2. Of those that a mesh axis runs over, the one named last changes fastest.
Arguments:
- a_tiles: bfloat16 [8, 2, 2, 8, 8, 128, 128], P(('groups', 'row'), 'col', None, None, 'layer'), parts along dimension 0, may hold values from -6 to 6
- a_offsets: int32 [8, 2, 2, 8, 8], P(('groups', 'row'), 'col', None, None, 'layer'), parts along dimension 0, may hold values from -2 to 2
- atom_owner: int32 [128], P(('groups', 'row', 'col')), parts along dimension 0, may hold values from 0 to 1, as said below
- b_tiles: bfloat16 [128, 12, 128, 128], P(('groups', 'row', 'col'), 'layer'), parts along dimension 0, may hold values from -0.5 to 0.5
- b_offsets: int32 [128, 12], P('groups'), parts along dimension 0, may hold values from -2 to 2
- c_offsets: int32 [128, 8], P(('groups', 'row', 'col')), parts along dimension 0, may hold values from -4 to 4
- block_sizes: int32 [128], P('groups'), parts along dimension 0, may hold values from 64 to 128
Outputs:
- c_tiles: bfloat16 [128, 8, 128, 128], P(('groups', 'row', 'col'), 'layer'), parts along dimension 0
The draws below stay inside these ranges and needn't reach their ends.
There are 2 independent parts, one for each index of `groups`. The reference program is written for one: setup_inputs(seed, part) draws one part's arguments, and reference() takes and returns one part's arrays. A program takes and returns all parts, laid end to end along the dimension named above; each array names one. Nothing has to cross between parts.
Inputs may be any that keep to these rules, and one draw needn't show every extreme that they name: `atom_owner`: in the atoms of one device (aligned blocks of 8 atoms) no owner holds more than 8 atoms, and some owner holds exactly 8.
All inputs are finite; a program needn't handle non-finite values.
Results may differ from the reference program's by a relative error of at most 0.001.
Values may be sent and summed in bfloat16 or wider, within the bound.
No kernel may reach another device: no remote copies, remote signals or barrier semaphores. Data moves between devices by JAX's collectives and lax.ppermute only.
A program may use at most 64 MiB of HBM per device.

```python
import jax
import jax.numpy as jnp
from jax import lax

TILE = 128
ATOMS_DEV = 8
A_SLOTS = 8
B_SLOTS = 12
C_SLOTS = 8
BAND = 2
BUCKET = 8
BLOCKS = 64
N_ROW = 4
N_COL = 2


def draw_atom_owner(key, part):
    key = jax.random.fold_in(key, 11)
    device_count = BLOCKS // ATOMS_DEV
    keys = jax.random.split(key, device_count)

    def one_device(sub_key):
        first_key, second_key, third_key = jax.random.split(sub_key, 3)
        leading = jax.random.randint(first_key, (), 0, N_COL)
        spread = jax.random.permutation(second_key, (N_COL - 1) * BUCKET)[:ATOMS_DEV - BUCKET]
        others = (leading + 1 + spread // BUCKET) % N_COL
        owners = jnp.concatenate([jnp.full((BUCKET,), leading, jnp.int32), others.astype(jnp.int32)])
        return jax.random.permutation(third_key, owners)
    return jax.vmap(one_device)(keys).reshape(-1).astype(jnp.int32)


def with_ends(drawn, own_key, least, top_value):
    dims = drawn.shape
    index_at = [jax.random.randint(jax.random.fold_in(own_key, axis), (), 0, dims[axis]) for axis in range(len(dims))]
    drawn = drawn.at[tuple(index_at)].set(least)
    longest = dims.index(max(dims))
    index_at[longest] = (index_at[longest] + 1) % dims[longest]
    return drawn.at[tuple(index_at)].set(top_value)


def shard_levels(stream_key, dims, cuts, least, top_value):
    def one(dim, blocks):
        heights = jax.random.uniform(jax.random.fold_in(jax.random.fold_in(stream_key, 6), dim), (blocks,), jnp.float32, least / len(cuts), top_value / len(cuts))
        return jnp.repeat(jnp.exp(heights), dims[dim] // blocks).reshape((-1,) + (1,) * (len(dims) - dim - 1))

    loudness = one(*cuts[0])
    for cut in cuts[1:]:
        loudness = loudness * one(*cut)
    return loudness


def centred(rng, extent, scale, limit, cuts=(), kind=jnp.bfloat16):
    loudness = shard_levels(rng, extent, cuts, -0.22, 0.18) if cuts else 1.0
    values = jax.random.normal(rng, extent, jnp.float32) * scale * loudness
    return jnp.minimum(jnp.maximum(values, -limit), limit).astype(kind)


def setup_inputs(seed: int = 0, part: int = 0) -> dict:
    splits = jax.random.split(jax.random.key(seed), 8)
    own_keys = jax.random.split(jax.random.fold_in(splits[7], part), 8)
    return {
        "a_tiles": centred(own_keys[0], (N_ROW, N_COL, N_COL, BUCKET, A_SLOTS, TILE, TILE), 1.0, 6.0, ((0, 4), (1, 2), (4, 2))),
        "a_offsets": with_ends(jax.random.randint(own_keys[1], (N_ROW, N_COL, N_COL, BUCKET, A_SLOTS), 0 - BAND, BAND + 1), jax.random.fold_in(own_keys[1], 1), 0 - BAND, BAND).astype(jnp.int32),
        "atom_owner": draw_atom_owner(jax.random.fold_in(jax.random.fold_in(splits[7], part), 71), part),
        "b_tiles": centred(own_keys[3], (BLOCKS, B_SLOTS, TILE, TILE), TILE ** -0.5, 0.5, ((0, 8), (1, 2))),
        "b_offsets": with_ends(jax.random.randint(own_keys[4], (BLOCKS, B_SLOTS), 0 - BAND, BAND + 1), jax.random.fold_in(own_keys[4], 1), 0 - BAND, BAND).astype(jnp.int32),
        "c_offsets": with_ends(jax.random.randint(own_keys[5], (BLOCKS, C_SLOTS), 0 - 2 * BAND, 2 * BAND + 1), jax.random.fold_in(own_keys[5], 1), 0 - 2 * BAND, 2 * BAND).astype(jnp.int32),
        "block_sizes": with_ends(jax.random.randint(own_keys[6], (BLOCKS,), TILE // 2, TILE + 1), jax.random.fold_in(own_keys[6], 1), TILE // 2, TILE).astype(jnp.int32),
    }


def reference(a_tiles, a_offsets, atom_owner, b_tiles, b_offsets, c_offsets, block_sizes):
    cycle_size = N_ROW * N_COL
    grouped = atom_owner.reshape(cycle_size, ATOMS_DEV)
    places = jnp.arange(ATOMS_DEV, dtype=jnp.int32)
    same_owner = grouped[:, :, None] == grouped[:, None, :]
    earlier = places[None, :] < places[:, None]
    owner_rank = jnp.sum(same_owner & earlier[None], axis=2).reshape(-1).astype(jnp.int32)
    atom_index = jnp.arange(BLOCKS, dtype=jnp.int32)
    groups = atom_index // (ATOMS_DEV * N_COL)
    target = (atom_index // ATOMS_DEV) % N_COL
    source = (((groups * N_COL + atom_owner) * N_COL + target) * BUCKET + owner_rank).astype(jnp.int32)
    a_full = jnp.take(a_tiles.reshape(-1, A_SLOTS, TILE, TILE), source, axis=0)
    a_shift = jnp.take(a_offsets.reshape(-1, A_SLOTS), source, axis=0)
    col_a = (atom_index[:, None] + a_shift) % BLOCKS
    col_b = (atom_index[:, None] + b_offsets) % BLOCKS
    col_c = (atom_index[:, None] + c_offsets) % BLOCKS
    row_iota = lax.broadcasted_iota(jnp.int32, (TILE, TILE), 0)
    col_iota = lax.broadcasted_iota(jnp.int32, (TILE, TILE), 1)
    size_inner = jnp.take(block_sizes, col_a)
    size_outer = jnp.take(block_sizes, col_b)
    keep_a = (row_iota < block_sizes[:, None, None, None]) & (col_iota < size_inner[:, :, None, None])
    masked_a = jnp.where(keep_a, a_full, jnp.zeros_like(a_full))
    keep_b = col_iota < size_outer[:, :, None, None]
    masked_b = jnp.where(keep_b, b_tiles, jnp.zeros_like(b_tiles))

    def one_row(row_id):
        inner = col_a[row_id]
        picked = jnp.take(masked_b, inner, axis=0).astype(jnp.float32)
        reached = jnp.take(col_b, inner, axis=0)
        matches = (col_c[row_id][:, None, None] == reached[None]).astype(jnp.float32)
        combined = jnp.einsum("stu,tuab->tsab", matches, picked, precision=lax.Precision.HIGHEST)
        left = masked_a[row_id].astype(jnp.float32)
        total = jnp.einsum("tab,tsbc->sac", left, combined, precision=lax.Precision.HIGHEST)
        return total.astype(jnp.bfloat16)

    return lax.map(one_row, atom_index)
```

```python
import functools

import jax
import jax.numpy as jnp
from jax import lax
from jax.experimental import pallas as pl
from jax.experimental.pallas import tpu as pltpu
from jax.sharding import PartitionSpec as P

BAND = 2
WIDTH = 2 * BAND + 1
SMEM = pl.BlockSpec(memory_space=pltpu.SMEM)
VMEM = pl.BlockSpec(memory_space=pltpu.VMEM)
HBM = pl.BlockSpec(memory_space=pl.ANY)


def band_kernel(pos, b_offsets, sizes, b_own, b_peer, table, tail, head, total):
    atoms, half, tile, _ = b_own.shape
    blocks = sizes.shape[0]
    start, layer = pos[0], pos[1]
    row_iota = lax.broadcasted_iota(jnp.int32, (tile, tile), 0)
    col_iota = lax.broadcasted_iota(jnp.int32, (tile, tile), 1)

    def one_row(k, _):
        for w in range(WIDTH):
            total[w] = jnp.zeros((tile, tile), jnp.float32)
        for part, ref in ((layer, b_own), (1 - layer, b_peer)):
            for j in range(half):
                w = b_offsets[k, part * half + j] + BAND
                total[w] = total[w] + ref[k, j].astype(jnp.float32)
        rows = sizes[start + k]
        for w in range(WIDTH):
            cols = sizes[lax.rem(start + k + w + blocks - BAND, blocks)]
            value = jnp.where((row_iota < rows) & (col_iota < cols), total[w], 0.0)
            high = value.astype(jnp.bfloat16)
            low = (value - high.astype(jnp.float32)).astype(jnp.bfloat16)
            table[k * WIDTH + w, 0:tile] = high
            table[k * WIDTH + w, tile : 2 * tile] = low
        return 0

    lax.fori_loop(0, atoms, one_row, 0)
    tail[...] = table[pl.ds((atoms - BAND + layer) * WIDTH, WIDTH)]
    head[...] = table[pl.ds(layer * WIDTH, WIDTH)]


def band_sums(pos, b_offsets, sizes, b_own, b_peer):
    atoms, half, tile, _ = b_own.shape
    shape = lambda rows: jax.ShapeDtypeStruct((rows * WIDTH, 2 * tile, tile), jnp.bfloat16)
    return pl.pallas_call(
        band_kernel,
        out_shape=(shape(atoms), shape(1), shape(1)),
        in_specs=[SMEM, SMEM, SMEM, VMEM, VMEM],
        out_specs=(VMEM, VMEM, VMEM),
        scratch_shapes=[pltpu.VMEM((WIDTH, tile, tile), jnp.float32)],
        compiler_params=pltpu.CompilerParams(vmem_limit_bytes=24 * 2**20),
        cost_estimate=pl.CostEstimate(flops=10**7, bytes_accessed=8 * 2**20, transcendentals=0),
        name="band_sums",
    )(pos, b_offsets, sizes, b_own, b_peer)


def product_kernel(runs, n_src, n_halo, dest, aliased, atoms, *refs):
    refs = list(refs)
    pos, owner, c_offsets, sizes = refs[:4]
    del refs[:4]
    shifts = [(refs[2 * i], refs[2 * i + 1]) for i in range(n_src)]
    del refs[: 2 * n_src]
    local = refs[:2]
    del refs[:2]
    n_chunks = max(r[2] for r in runs) + 1 if n_src == 2 else 0
    chunks = [(refs[2 * i], refs[2 * i + 1]) for i in range(n_chunks)]
    del refs[: 2 * n_chunks]
    table = refs.pop(0)
    halo = refs[:n_halo]
    del refs[:n_halo]
    if aliased:
        refs.pop(0)
    out, a_v, t_v, o_v, a_sem, t_sem, o_sem = refs
    start, layer, me = pos[0], pos[1], pos[2]
    d = me if dest is None else dest
    half = shifts[0][0].shape[-1]
    slots = o_v.shape[1]
    tile = o_v.shape[2]
    mine = owner[0] == me if n_src == 2 else None
    zero_at = (atoms + 2 * BAND) * WIDTH

    first = min(r[0] for r in runs)
    last = max(r[0] + r[1] for r in runs) + 2 * BAND
    if n_halo:
        first, last = 0, atoms + 2 * BAND
    low, high = max(first, BAND), min(last, atoms + BAND)
    fills = [
        pltpu.make_async_copy(
            table.at[pl.ds((low - BAND) * WIDTH, (high - low) * WIDTH)],
            t_v.at[pl.ds(low * WIDTH, (high - low) * WIDTH)],
            t_sem.at[0],
        )
    ]
    if n_halo:
        places = (layer, 1 - layer, atoms + BAND + layer, atoms + BAND + 1 - layer)
        for i, (ref, place) in enumerate(zip(halo, places, strict=True)):
            fills.append(
                pltpu.make_async_copy(ref, t_v.at[pl.ds(place * WIDTH, WIDTH)], t_sem.at[1 + i])
            )
    base = 0
    for p0, count, chunk, at in runs:

        def fetch(n, _, p0=p0, chunk=chunk, at=at, base=base):
            def begin(src):
                for h in range(2):
                    pltpu.make_async_copy(
                        src[h], a_v.at[base + n, pl.ds(h * half, half)], a_sem.at[base + n, h]
                    ).start()

            here = (local[0].at[0, 0, d, p0 + n], local[1].at[p0 + n])
            if n_src == 2:
                pl.when(mine)(lambda: begin(here))
                pl.when(jnp.logical_not(mine))(
                    lambda: begin((chunks[chunk][0].at[at + n], chunks[chunk][1].at[at + n]))
                )
            else:
                begin(here)
            return 0

        lax.fori_loop(0, count, fetch, 0)
        base += count
    for fill in fills:
        fill.start()
    t_v[zero_at] = jnp.zeros(t_v.shape[1:], t_v.dtype)
    for fill in fills:
        fill.wait()
    row_iota = lax.broadcasted_iota(jnp.int32, (tile, slots * tile // 2), 0)
    base = 0
    for p0, count, _, _ in runs:

        def one_atom(n, _, p0=p0, base=base):
            p = p0 + n
            for h in range(2):
                pltpu.make_async_copy(
                    local[1].at[p], a_v.at[base + n, pl.ds(h * half, half)], a_sem.at[base + n, h]
                ).wait()
            reach = []
            for h in range(2):
                for t in range(half):
                    if n_src == 2:
                        shift = jnp.where(
                            mine, shifts[0][h][0, 0, d, p, t], shifts[1][h][0, 0, d, p, t]
                        )
                    else:
                        shift = shifts[0][h][0, 0, d, p, t]
                    reach.append(shift)
            wanted = [c_offsets[p, layer * slots + s] for s in range(slots)]
            size = sizes[start + p]

            def place(t, s):
                w = wanted[s] - reach[t] + BAND
                at = (p + BAND + reach[t]) * WIDTH + w
                return jnp.where((w >= 0) & (w < WIDTH), at, zero_at)

            for pair in range(slots // 2):
                total = jnp.zeros((tile, 2 * tile), jnp.float32)
                for t in range(2 * half):
                    left = a_v[base + n, t]
                    left = jnp.concatenate([left, left], axis=1)
                    right = jnp.concatenate(
                        [t_v[place(t, 2 * pair)], t_v[place(t, 2 * pair + 1)]], axis=1
                    )
                    total += jnp.dot(left, right, preferred_element_type=jnp.float32)
                total = jnp.where(row_iota < size, total, 0.0).astype(jnp.bfloat16)
                o_v[base + n, 2 * pair] = total[:, :tile]
                o_v[base + n, 2 * pair + 1] = total[:, tile:]
            pltpu.make_async_copy(o_v.at[base + n], out.at[p], o_sem.at[base + n]).start()
            return 0

        lax.fori_loop(0, count, one_atom, 0)
        base += count
    base = 0
    for p0, count, _, _ in runs:

        def finish(n, _, p0=p0, base=base):
            pltpu.make_async_copy(o_v.at[base + n], out.at[p0 + n], o_sem.at[base + n]).wait()
            return 0

        lax.fori_loop(0, count, finish, 0)
        base += count


def products(runs, scalars, shifts, local, chunks, table, halo, slots, dest, prior):
    atoms = local[1].shape[0]
    _, half, tile, _ = local[1].shape
    count = sum(r[1] for r in runs)
    operands = list(scalars) + [s for pair in shifts for s in pair] + list(local)
    operands += [c for pair in chunks for c in pair] + [table] + list(halo)
    specs = [SMEM] * (4 + 2 * len(shifts)) + [HBM] * (len(operands) - 4 - 2 * len(shifts))
    aliases = {}
    if prior is not None:
        aliases = {len(operands): 0}
        operands.append(prior)
        specs.append(HBM)
    kernel = functools.partial(
        product_kernel, runs, len(shifts), len(halo), dest, prior is not None, atoms
    )
    return pl.pallas_call(
        kernel,
        out_shape=jax.ShapeDtypeStruct((atoms, slots, tile, tile), jnp.bfloat16),
        in_specs=specs,
        out_specs=HBM,
        scratch_shapes=[
            pltpu.VMEM((count, 2 * half, tile, tile), jnp.bfloat16),
            pltpu.VMEM(((atoms + 2 * BAND) * WIDTH + 1, 2 * tile, tile), jnp.bfloat16),
            pltpu.VMEM((count, slots, tile, tile), jnp.bfloat16),
            pltpu.SemaphoreType.DMA((count, 2)),
            pltpu.SemaphoreType.DMA((5,)),
            pltpu.SemaphoreType.DMA((count,)),
        ],
        input_output_aliases=aliases,
        compiler_params=pltpu.CompilerParams(vmem_limit_bytes=24 * 2**20),
        cost_estimate=pl.CostEstimate(
            flops=count * 2 * tile**3 * 4 * half * slots,
            bytes_accessed=4 * 2**20,
            transcendentals=0,
        ),
        name="products",
    )(*operands)


def local(a_tiles, a_offsets, atom_owner, b_tiles, b_offsets, c_offsets, block_sizes):
    cols = lax.axis_size("col")
    cycle = lax.axis_size("row") * cols
    atoms = atom_owner.shape[0]
    bucket = a_tiles.shape[3]
    slots = c_offsets.shape[1] // 2
    me = lax.axis_index("col")
    layer = lax.axis_index("layer")
    start = (lax.axis_index("row") * cols + me) * atoms
    pos = jnp.stack([start, layer, me]).astype(jnp.int32)
    assert atoms * cycle > 8 * BAND and lax.axis_size("layer") == 2 and atoms >= 2 * BAND

    def across(x):
        return lax.ppermute(x, "layer", [(0, 1), (1, 0)])

    def swap(x):
        return lax.ppermute(x, "col", [(0, 1), (1, 0)])

    def onward(x):
        return lax.ppermute(x, ("row", "col"), [(i, (i + 1) % cycle) for i in range(cycle)])

    def back(x):
        return lax.ppermute(x, ("row", "col"), [((i + 1) % cycle, i) for i in range(cycle)])

    whole = cols == 2 and bucket == atoms and atoms == 8
    if whole:
        def part(p0, count):
            at = (0, 0, 1 - me, p0, 0, 0, 0)
            size = (1, 1, 1, count) + a_tiles.shape[4:]
            return lax.dynamic_slice(a_tiles, at, size).reshape((count,) + a_tiles.shape[4:])

        far = [swap(part(0, 4)), swap(part(6, 2))]
    b_peer = across(b_tiles)
    own_rows = lax.dynamic_slice_in_dim(b_offsets, start, atoms, 0)
    table, tail, head = band_sums(pos, own_rows, block_sizes, b_tiles, b_peer)
    if whole:
        rest = part(4, 2)
        tail, head, rest = lax.optimization_barrier((tail, head, rest))
    tail, head = onward(tail), back(head)
    scalars = (pos, atom_owner, c_offsets, block_sizes)
    if whole:
        far.append(swap(rest))
        shifts = [a_offsets, swap(a_offsets)]
        shifts = [(s, across(s)) for s in shifts]
        near = lax.dynamic_index_in_dim(a_tiles[0, 0], me, 0, keepdims=False)
        held = (a_tiles, across(near))
        far = [(f, across(f)) for f in far]
        halo = (tail, across(tail), head, across(head))
        call = functools.partial(
            products, scalars=scalars, shifts=shifts, local=held, table=table, slots=slots
        )
        c = call([(2, 2, 0, 2)], chunks=far[:1], halo=(), dest=None, prior=None)
        c = call(
            [(0, 2, 0, 0), (6, 2, 1, 0)], chunks=far[:2], halo=halo, dest=None, prior=c
        )
        return call([(4, 2, 0, 0)], chunks=far[2:], halo=(), dest=None, prior=c)
    received = lax.all_to_all(a_tiles, "col", split_axis=2, concat_axis=1, tiled=True)
    moved = lax.all_to_all(a_offsets, "col", split_axis=2, concat_axis=1, tiled=True)
    received = received.reshape((-1,) + received.shape[4:])
    moved = moved.reshape((-1,) + moved.shape[4:])
    places = jnp.arange(atoms, dtype=jnp.int32)
    same = atom_owner[:, None] == atom_owner[None, :]
    rank = jnp.sum(same & (places[None, :] < places[:, None]), axis=1)
    source = atom_owner * bucket + rank
    rows = jnp.take(received, source, axis=0)
    shift = jnp.take(moved, source, axis=0)[None, None, None]
    halo = (tail, across(tail), head, across(head))
    return products(
        [(0, atoms, 0, 0)],
        scalars,
        [(shift, across(shift))],
        (rows[None, None, None], across(rows)),
        [],
        table,
        halo,
        slots,
        0,
        None,
    )


def solution(mesh):
    placed = (
        P(("groups", "row"), "col", None, None, "layer", None, None),
        P(("groups", "row"), "col", None, None, "layer"),
        P(("groups", "row", "col")),
        P(("groups", "row", "col"), "layer", None, None),
        P("groups", None),
        P(("groups", "row", "col"), None),
        P("groups"),
    )
    return jax.shard_map(
        local,
        mesh=mesh,
        in_specs=placed,
        out_specs=P(("groups", "row", "col"), "layer", None, None),
        check_vma=False,
    )
```

```python
import functools

import jax
import jax.numpy as jnp
from jax import lax
from jax.experimental import pallas as pl
from jax.experimental.pallas import tpu as pltpu
from jax.sharding import PartitionSpec as P

BAND = 2
WIDTH = 2 * BAND + 1
SMEM = pl.BlockSpec(memory_space=pltpu.SMEM)
VMEM = pl.BlockSpec(memory_space=pltpu.VMEM)
ANY = pl.BlockSpec(memory_space=pl.ANY)


def settings(mib):
    return dict(
        compiler_params=pltpu.CompilerParams(vmem_limit_bytes=mib * 2**20),
        cost_estimate=pl.CostEstimate(flops=1, bytes_accessed=1, transcendentals=0),
    )


def cut_kernel(cuts, more, a_tiles, *refs):
    n = len(cuts)
    a_offsets = refs[0]
    outs, bounces, (in_sem, out_sem) = refs[-2 - 2 * n : -2 - n], refs[-2 - n : -2], refs[-2:]
    half, tile = a_tiles.shape[4:6]
    other = 1 - lax.axis_index("col")
    ins, back = [], []
    for i, (p0, count) in enumerate(cuts):
        ins.append(
            [
                pltpu.make_async_copy(
                    a_tiles.at[0, 0, other, p0 + j],
                    bounces[i].at[pl.ds(j * half, half)],
                    in_sem.at[i, j],
                )
                for j in range(count)
            ]
        )
        back.append(pltpu.make_async_copy(bounces[i], outs[i], out_sem.at[i]))
    for moves in ins:
        for move in moves:
            move.start()
    if more:
        atoms = a_offsets.shape[3]
        values = a_offsets[0, 0, pl.ds(other, 1)].reshape(atoms, half).astype(jnp.float32)
        values = jnp.pad(values, ((0, 16 - atoms), (0, tile - half)))
        bounces[0][cuts[0][1] * half, 0:16] = values.astype(jnp.bfloat16)
    for moves, move_back in zip(ins, back, strict=True):
        for move in moves:
            move.wait()
        move_back.start()
    for move in back:
        move.wait()


def cut(a_tiles, cuts, more=()):
    half, tile = a_tiles.shape[4:6]
    n = len(cuts)
    shapes = [(c * half + (bool(more) and i == 0), tile, tile) for i, (_, c) in enumerate(cuts)]
    return pl.pallas_call(
        functools.partial(cut_kernel, cuts, bool(more)),
        out_shape=tuple(jax.ShapeDtypeStruct(s, a_tiles.dtype) for s in shapes),
        in_specs=[ANY] + [VMEM, ANY][: len(more)],
        out_specs=(ANY,) * n,
        scratch_shapes=[pltpu.VMEM(s, a_tiles.dtype) for s in shapes]
        + [
            pltpu.SemaphoreType.DMA((n, max(c for _, c in cuts))),
            pltpu.SemaphoreType.DMA((n,)),
        ],
        name="cut",
        **settings(56),
    )(a_tiles, *more)


def band_kernel(b_offsets, sizes, place, b_own, b_peer, table, tail, head, total):
    atoms, half, tile, _ = b_own.shape
    blocks = sizes.shape[0]
    start, layer = place[0], place[1]
    row_iota = lax.broadcasted_iota(jnp.int32, (tile, tile), 0)
    col_iota = lax.broadcasted_iota(jnp.int32, (tile, tile), 1)

    def one_row(k, _):
        for w in range(WIDTH):
            total[w] = jnp.zeros((tile, tile), jnp.float32)
        for part, ref in ((layer, b_own), (1 - layer, b_peer)):
            for j in range(half):
                w = b_offsets[k, part * half + j] + BAND
                total[w] = total[w] + ref[k, j].astype(jnp.float32)
        rows = sizes[start + k]
        for w in range(WIDTH):
            cols = sizes[lax.rem(start + k + w + blocks - BAND, blocks)]
            value = jnp.where((row_iota < rows) & (col_iota < cols), total[w], 0.0)
            high = value.astype(jnp.bfloat16)
            table[2 * (k * WIDTH + w)] = high
            table[2 * (k * WIDTH + w) + 1] = (value - high.astype(jnp.float32)).astype(jnp.bfloat16)
        return 0

    lax.fori_loop(0, atoms, one_row, 0)
    pair = 2 * WIDTH
    table[pl.ds(atoms * pair, 2)] = jnp.zeros((2, tile, tile), table.dtype)
    tail[...] = table[pl.ds((atoms - BAND + layer) * pair, pair)]
    head[...] = table[pl.ds(layer * pair, pair)]


def band_sums(b_offsets, sizes, place, b_own, b_peer):
    atoms, half, tile, _ = b_own.shape
    shape = lambda tiles: jax.ShapeDtypeStruct((tiles, tile, tile), jnp.bfloat16)
    return pl.pallas_call(
        band_kernel,
        out_shape=(shape(2 * (atoms * WIDTH + 1)), shape(2 * WIDTH), shape(2 * WIDTH)),
        in_specs=[SMEM, SMEM, SMEM, VMEM, VMEM],
        out_specs=(VMEM, VMEM, VMEM),
        scratch_shapes=[pltpu.VMEM((WIDTH, tile, tile), jnp.float32)],
        name="band_sums",
        **settings(16),
    )(b_offsets, sizes, place, b_own, b_peer)


def plan_kernel(two, slots, owner, c_offsets, sizes, place, *refs):
    shifts, far, out = refs[:2], refs[2:4] if two else (), refs[4 if two else 2]
    atoms, half = shifts[0].shape[-2:]
    start, layer, me = place[0], place[1], place[2]
    d = me if two else 0
    mine = owner[0] == me
    if two:
        raw, whole, as_int, sem = refs[5:]
        moves = [
            pltpu.make_async_copy(ref.at[ref.shape[0] - 1, pl.ds(0, 16)], raw.at[h], sem.at[h])
            for h, ref in enumerate(far)
        ]
        for move in moves:
            move.start()
        for move in moves:
            move.wait()
        whole[...] = raw[...].astype(jnp.float32).astype(jnp.int32)
        move = pltpu.make_async_copy(whole, as_int, sem.at[0])
        move.start()
        move.wait()
    out[atoms, 0] = layer
    out[atoms, 1] = me
    out[atoms, 2] = mine.astype(jnp.int32)

    def one_atom(p, _):
        out[p, 2 * half * slots] = sizes[start + p]
        wanted = [c_offsets[p, layer * slots + s] for s in range(slots)]
        for h in range(2):
            for t in range(half):
                shift = shifts[h][0, 0, d, p, t]
                if two:
                    shift = jnp.where(mine, shift, as_int[h, p, t])
                for s in range(slots):
                    w = wanted[s] - shift + BAND
                    at = (p + BAND + shift) * WIDTH + w
                    out[p, (h * half + t) * slots + s] = jnp.where(
                        (w >= 0) & (w < WIDTH), at, -1
                    )
        return 0

    lax.fori_loop(0, atoms, one_atom, 0)


def make_plan(owner, c_offsets, sizes, place, shifts, slots, far=()):
    atoms, half = shifts[0].shape[-2:]
    scratch = []
    if far:
        tile = far[0].shape[-1]
        scratch = [
            pltpu.VMEM((2, 16, tile), jnp.bfloat16),
            pltpu.VMEM((2, 16, tile), jnp.int32),
            pltpu.SMEM((2, 16, tile), jnp.int32),
            pltpu.SemaphoreType.DMA((2,)),
        ]
    return pl.pallas_call(
        functools.partial(plan_kernel, bool(far), slots),
        out_shape=jax.ShapeDtypeStruct((atoms + 1, 2 * half * slots + 1), jnp.int32),
        in_specs=[SMEM] * 6 + [ANY] * len(far),
        out_specs=SMEM,
        scratch_shapes=scratch,
        name="plan",
        **settings(4),
    )(owner, c_offsets, sizes, place, *shifts, *far)


def product_kernel(cfg, plan, *refs):
    refs = list(refs)
    near = refs[:2]
    del refs[:2]
    far = [refs[2 * i : 2 * i + 2] for i in range(cfg["n_far"])]
    del refs[: 2 * cfg["n_far"]]
    table = refs.pop(0)
    halo = refs[: cfg["n_halo"]]
    del refs[: cfg["n_halo"]]
    if cfg["aliased"]:
        refs.pop(0)
    out, a_v, t_v, o_v, a_sem, t_sem, o_sem = refs
    atoms, p0, side = cfg["atoms"], cfg["p0"], cfg["side"]
    count, slots, tile, _ = o_v.shape
    half = a_v.shape[1] // 2
    layer, me, mine = plan[atoms, 0], plan[atoms, 1], plan[atoms, 2]
    d = me if far else 0
    batch = count // max(len(far), 1)

    def moves(n, src):
        if src == 0:
            found = [near[h].at[0, 0, d, p0 + n] for h in range(2)]
        else:
            found = [far[n // batch][h].at[pl.ds(n % batch * half, half)] for h in range(2)]
        return [
            pltpu.make_async_copy(found[h], a_v.at[n, pl.ds(h * half, half)], a_sem.at[n, h])
            for h in range(2)
        ]

    def begin(src):
        for n in range(count):
            for move in moves(n, src):
                move.start()

    if far:
        pl.when(mine == 1)(lambda: begin(0))
        pl.when(mine != 1)(lambda: begin(1))
    else:
        begin(0)
    row0 = BAND
    tiles = table
    if side is not None:
        pair = 2 * WIDTH
        rows = 3 * BAND
        own, own_at, halo_at, row0 = (
            (0, BAND, 0, 0) if side == "low" else (atoms - 2 * BAND, 0, 2 * BAND, atoms - BAND)
        )
        tiles = t_v
        fills = [
            pltpu.make_async_copy(
                table.at[pl.ds(own * pair, 2 * BAND * pair)],
                t_v.at[pl.ds(own_at * pair, 2 * BAND * pair)],
                t_sem.at[0],
            )
        ]
        for i, ref in enumerate(halo):
            at = halo_at + (layer if i == 0 else 1 - layer)
            fills.append(
                pltpu.make_async_copy(ref, t_v.at[pl.ds(at * pair, pair)], t_sem.at[1 + i])
            )
        for fill in fills:
            fill.start()
        t_v[pl.ds(rows * pair, 2)] = jnp.zeros((2, tile, tile), t_v.dtype)
        for fill in fills:
            fill.wait()
    zero_at = tiles.shape[0] // 2 - 1
    row_iota = lax.broadcasted_iota(jnp.int32, (tile, 2 * tile), 0)

    def one_atom(n, _):
        p = p0 + n
        for move in moves(n, 0):
            move.wait()

        def factor(t, s):
            at = plan[p, t * slots + s]
            at = 2 * jnp.where(at < 0, zero_at, at - row0 * WIDTH)
            return jnp.concatenate([tiles[at], tiles[at + 1]], axis=0)

        size = plan[p, 2 * half * slots]
        for q in range(slots // 2):
            total = jnp.zeros((tile, 2 * tile), jnp.float32)
            for t in range(2 * half):
                left = a_v[n, t]
                left = jnp.concatenate([left, left], axis=1)
                right = jnp.concatenate([factor(t, 2 * q), factor(t, 2 * q + 1)], axis=1)
                total += jnp.dot(left, right, preferred_element_type=jnp.float32)
            total = jnp.where(row_iota < size, total, 0.0).astype(jnp.bfloat16)
            o_v[n, 2 * q] = total[:, :tile]
            o_v[n, 2 * q + 1] = total[:, tile:]
        pltpu.make_async_copy(o_v.at[n], out.at[p], o_sem.at[n]).start()
        return 0

    lax.fori_loop(0, count, one_atom, 0)

    def finish(n, _):
        pltpu.make_async_copy(o_v.at[n], out.at[p0 + n], o_sem.at[n]).wait()
        return 0

    lax.fori_loop(0, count, finish, 0)


def products(plan, near, far, table, halo, side, slots, atoms, prior=None):
    tile, half = table.shape[-1], near[0].shape[-3]
    count = atoms - 2 * BAND if side is None else BAND
    operands = [plan, *near, *[f for pair in far for f in pair], table, *halo]
    specs = [SMEM] + [ANY] * (len(operands) - 1)
    specs[1 + 2 + 2 * len(far)] = VMEM
    aliases = {}
    if prior is not None:
        aliases = {len(operands): 0}
        operands.append(prior)
        specs.append(ANY)
    cfg = dict(
        atoms=atoms,
        p0={None: BAND, "low": 0, "top": atoms - BAND}[side],
        n_far=len(far),
        n_halo=len(halo),
        side=side,
        aliased=prior is not None,
    )
    rows = 0 if side is None else 3 * BAND * WIDTH
    return pl.pallas_call(
        functools.partial(product_kernel, cfg),
        out_shape=jax.ShapeDtypeStruct((atoms, slots, tile, tile), jnp.bfloat16),
        in_specs=specs,
        out_specs=ANY,
        scratch_shapes=[
            pltpu.VMEM((count, 2 * half, tile, tile), jnp.bfloat16),
            pltpu.VMEM((2 * (rows + 1), tile, tile), jnp.bfloat16),
            pltpu.VMEM((count, slots, tile, tile), jnp.bfloat16),
            pltpu.SemaphoreType.DMA((count, 2)),
            pltpu.SemaphoreType.DMA((3,)),
            pltpu.SemaphoreType.DMA((count,)),
        ],
        input_output_aliases=aliases,
        name="products" if side is None else "products_" + side,
        **settings(12),
    )(*operands)


def after(x, *others):
    return lax.optimization_barrier((x,) + others)[0]


def local(a_tiles, a_offsets, atom_owner, b_tiles, b_offsets, c_offsets, block_sizes):
    cols = lax.axis_size("col")
    cycle = lax.axis_size("row") * cols
    atoms = atom_owner.shape[0]
    bucket = a_tiles.shape[3]
    slots = c_offsets.shape[1] // 2
    me = lax.axis_index("col")
    layer = lax.axis_index("layer")
    start = (lax.axis_index("row") * cols + me) * atoms
    place = jnp.stack([start, layer, me]).astype(jnp.int32)
    assert atoms * cycle > 8 * BAND and lax.axis_size("layer") == 2 and atoms >= 4 * BAND

    def across(x):
        return lax.ppermute(x, "layer", [(0, 1), (1, 0)])

    def swap(x):
        return lax.ppermute(x, "col", [(0, 1), (1, 0)])

    def onward(x):
        return lax.ppermute(x, ("row", "col"), [(i, (i + 1) % cycle) for i in range(cycle)])

    def back(x):
        return lax.ppermute(x, ("row", "col"), [((i + 1) % cycle, i) for i in range(cycle)])

    b_peer = across(b_tiles)
    if cols == 2 and bucket == atoms:
        firsts = cut(a_tiles, ((BAND, BAND),))
        rest = ((2 * BAND, atoms - 3 * BAND), (0, BAND), (atoms - BAND, BAND))
        mid, low, top = cut(a_tiles, rest, (a_offsets, firsts[0]))
        b_offsets = after(b_offsets, mid)
        near = (a_tiles, across(after(a_tiles, mid)))
        mids = [swap(firsts[0]), swap(mid)]
    own_rows = lax.dynamic_slice_in_dim(b_offsets, start, atoms, 0)
    table, tail, head = band_sums(own_rows, block_sizes, place, b_tiles, b_peer)
    tail, head = onward(tail), back(head)
    if cols == 2 and bucket == atoms:
        low, top = swap(after(low, table)), swap(after(top, table))
        mids = [after(m, table) for m in mids]
        mids = [(m, across(m)) for m in mids]
        shifts = (a_offsets, across(a_offsets))
        plan = make_plan(atom_owner, c_offsets, block_sizes, place, shifts, slots, mids[-1])
        call = functools.partial(products, plan, near, slots=slots, atoms=atoms)
        c = call(mids, table, (), None)
        tail, head = after(tail, c), after(head, c)
        tail, head = (tail, across(tail)), (head, across(head))
        low = ((low, across(low)),)
        c = call(low, table, tail, "low", prior=c)
        top = after(top, c, head[1])
        return call(((top, across(top)),), table, head, "top", prior=c)
    received = lax.all_to_all(a_tiles, "col", split_axis=2, concat_axis=1, tiled=True)
    moved = lax.all_to_all(a_offsets, "col", split_axis=2, concat_axis=1, tiled=True)
    received = received.reshape((-1,) + received.shape[4:])
    moved = moved.reshape((-1,) + moved.shape[4:])
    places = jnp.arange(atoms, dtype=jnp.int32)
    same = atom_owner[:, None] == atom_owner[None, :]
    rank = jnp.sum(same & (places[None, :] < places[:, None]), axis=1)
    source = atom_owner * bucket + rank
    rows = jnp.take(received, source, axis=0)[None, None, None]
    shift = jnp.take(moved, source, axis=0)[None, None, None]
    plan = make_plan(atom_owner, c_offsets, block_sizes, place, (shift, across(shift)), slots)
    call = functools.partial(
        products, plan, (rows, across(rows)), [], table, slots=slots, atoms=atoms
    )
    c = call((), None)
    c = call((tail, across(tail)), "low", prior=c)
    return call((head, across(head)), "top", prior=c)


def solution(mesh):
    placed = (
        P(("groups", "row"), "col", None, None, "layer", None, None),
        P(("groups", "row"), "col", None, None, "layer"),
        P(("groups", "row", "col")),
        P(("groups", "row", "col"), "layer", None, None),
        P("groups", None),
        P(("groups", "row", "col"), None),
        P("groups"),
    )
    return jax.shard_map(
        local,
        mesh=mesh,
        in_specs=placed,
        out_specs=P(("groups", "row", "col"), "layer", None, None),
        check_vma=False,
    )
```

```python
import functools

import jax
import jax.numpy as jnp
from jax import lax
from jax.experimental import pallas as pl
from jax.experimental.pallas import tpu as pltpu
from jax.sharding import PartitionSpec as P

BAND = 2
WIDTH = 2 * BAND + 1
SMEM = pl.BlockSpec(memory_space=pltpu.SMEM)
VMEM = pl.BlockSpec(memory_space=pltpu.VMEM)
ANY = pl.BlockSpec(memory_space=pl.ANY)


def settings(mib):
    return dict(
        compiler_params=pltpu.CompilerParams(vmem_limit_bytes=mib * 2**20),
        cost_estimate=pl.CostEstimate(flops=1, bytes_accessed=1, transcendentals=0),
    )


def cut_kernel(cuts, away, more, a_rows, *refs):
    n = len(cuts)
    offsets = refs[0]
    raw, in_sem, out_sem = refs[-3:]
    outs, bounces = refs[-3 - 2 * n : -3 - n], refs[-3 - n : -3]
    height, tile = a_rows.shape[4:]
    me = lax.axis_index("col")
    d = 1 - me if away else me
    ins, back = [], []
    for i, chosen in enumerate(cuts):
        ins.append(
            [
                pltpu.make_async_copy(
                    a_rows.at[0, 0, d, p],
                    bounces[i].at[pl.ds(j * height, height)],
                    in_sem.at[i, j],
                )
                for j, p in enumerate(chosen)
            ]
        )
        back.append(pltpu.make_async_copy(bounces[i], outs[i], out_sem.at[i]))
    for moves in ins:
        for move in moves:
            move.start()
    if more:
        half, atoms = offsets.shape[3:]
        move = pltpu.make_async_copy(offsets.at[0, 0, d], raw, out_sem.at[0])
        move.start()
        move.wait()
        values = jnp.pad(raw[...].astype(jnp.float32), ((0, 16 - half), (0, tile - atoms)))
        bounces[-1][pl.ds(len(cuts[-1]) * height, 16)] = values.astype(jnp.bfloat16)
    for moves, move_back in zip(ins, back, strict=True):
        for move in moves:
            move.wait()
        move_back.start()
    for move in back:
        move.wait()


def cut(a_rows, cuts, mib, away=True, offsets=None, earlier=()):
    height, tile = a_rows.shape[4:]
    n = len(cuts)
    more = offsets is not None
    shapes = [(len(c) * height + 16 * (more and i == n - 1), tile) for i, c in enumerate(cuts)]
    return pl.pallas_call(
        functools.partial(cut_kernel, cuts, away, more),
        out_shape=tuple(jax.ShapeDtypeStruct(s, a_rows.dtype) for s in shapes),
        in_specs=[ANY] + [ANY] * more + [ANY] * len(earlier),
        out_specs=(ANY,) * n,
        scratch_shapes=[pltpu.VMEM(s, a_rows.dtype) for s in shapes]
        + [
            pltpu.VMEM(offsets.shape[3:] if more else (8, 128), jnp.int32),
            pltpu.SemaphoreType.DMA((n, max(map(len, cuts)))),
            pltpu.SemaphoreType.DMA((n,)),
        ],
        name="cut",
        **settings(mib),
    )(a_rows, *([offsets] if more else []), *earlier)


def choose_kernel(chosen, owner, a_rows, offsets, far, first, second, raw, sem):
    height, tile = a_rows.shape[4:]
    me = lax.axis_index("col")
    mine = owner[0] == me
    split = first.shape[0] // height
    count = len(chosen)

    def run(here):
        if here:
            pairs = []
            for i, p in enumerate(chosen):
                out, at = (first, i) if i < split else (second, i - split)
                pairs.append((a_rows.at[0, 0, me, p], out.at[pl.ds(at * height, height)]))
        else:
            pairs = [
                (far.at[pl.ds(0, split * height)], first),
                (far.at[pl.ds(split * height, second.shape[0])], second),
            ]
        moves = [pltpu.make_async_copy(*p, sem.at[i]) for i, p in enumerate(pairs)]
        for move in moves:
            move.start()
        if here:
            half, atoms = offsets.shape[3:]
            move = pltpu.make_async_copy(offsets.at[0, 0, me], raw, sem.at[count])
            move.start()
            move.wait()
            values = jnp.pad(raw[...].astype(jnp.float32), ((0, 16 - half), (0, tile - atoms)))
            second[pl.ds((count - split) * height, 16)] = values.astype(second.dtype)
        for move in moves:
            move.wait()

    pl.when(mine)(lambda: run(True))
    pl.when(jnp.logical_not(mine))(lambda: run(False))


def choose(owner, a_rows, offsets, far, chosen):
    height, tile = a_rows.shape[4:]
    one = len(chosen) // 2 * height
    shape = lambda n: jax.ShapeDtypeStruct((n, tile), a_rows.dtype)
    return pl.pallas_call(
        functools.partial(choose_kernel, chosen),
        out_shape=(shape(one), shape(far.shape[0] - one)),
        in_specs=[SMEM, ANY, ANY, ANY],
        out_specs=(VMEM, VMEM),
        scratch_shapes=[
            pltpu.VMEM(offsets.shape[3:], jnp.int32),
            pltpu.SemaphoreType.DMA((len(chosen) + 1,)),
        ],
        name="choose",
        **settings(8),
    )(owner, a_rows, offsets, far)


def band_kernel(b_offsets, sizes, place, b_own, b_peer, table, tail, head, total):
    atoms, half, tile, _ = b_own.shape
    blocks = sizes.shape[0]
    start, layer = place[0], place[1]
    row_iota = lax.broadcasted_iota(jnp.int32, (tile, tile), 0)
    col_iota = lax.broadcasted_iota(jnp.int32, (tile, tile), 1)

    def one_row(k, _):
        for w in range(WIDTH):
            total[w] = jnp.zeros((tile, tile), jnp.float32)
        for part, ref in ((layer, b_own), (1 - layer, b_peer)):
            for j in range(half):
                w = b_offsets[k, part * half + j] + BAND
                total[w] = total[w] + ref[k, j].astype(jnp.float32)
        rows = sizes[start + k]
        for w in range(WIDTH):
            cols = sizes[lax.rem(start + k + w + blocks - BAND, blocks)]
            value = jnp.where((row_iota < rows) & (col_iota < cols), total[w], 0.0)
            high = value.astype(jnp.bfloat16)
            table[2 * (k * WIDTH + w)] = high
            table[2 * (k * WIDTH + w) + 1] = (value - high.astype(jnp.float32)).astype(jnp.bfloat16)
        return 0

    lax.fori_loop(0, atoms, one_row, 0)
    pair = 2 * WIDTH
    table[pl.ds(atoms * pair, 2)] = jnp.zeros((2, tile, tile), table.dtype)
    tail[...] = table[pl.ds((atoms - BAND + layer) * pair, pair)]
    head[...] = table[pl.ds(layer * pair, pair)]


def band_sums(b_offsets, sizes, place, b_own, b_peer):
    atoms, half, tile, _ = b_own.shape
    shape = lambda tiles: jax.ShapeDtypeStruct((tiles, tile, tile), jnp.bfloat16)
    return pl.pallas_call(
        band_kernel,
        out_shape=(shape(2 * (atoms * WIDTH + 1)), shape(2 * WIDTH), shape(2 * WIDTH)),
        in_specs=[SMEM, SMEM, SMEM, VMEM, VMEM],
        out_specs=(VMEM, VMEM, VMEM),
        scratch_shapes=[pltpu.VMEM((WIDTH, tile, tile), jnp.float32)],
        name="band_sums",
        **settings(16),
    )(b_offsets, sizes, place, b_own, b_peer)


def join_kernel(table, tail, other_tail, head, other_head, out, sem):
    layer = lax.axis_index("layer")
    pair = 2 * WIDTH
    rows = table.shape[0] // pair
    parts = (
        (table.at[pl.ds(0, rows * pair)], BAND, rows),
        (tail, layer, 1),
        (other_tail, 1 - layer, 1),
        (head, BAND + rows + layer, 1),
        (other_head, BAND + rows + 1 - layer, 1),
    )
    moves = [
        pltpu.make_async_copy(src, out.at[pl.ds(at * pair, n * pair)], sem.at[i])
        for i, (src, at, n) in enumerate(parts)
    ]
    for move in moves:
        move.start()
    out[pl.ds((rows + 2 * BAND) * pair, 2)] = jnp.zeros((2,) + out.shape[1:], out.dtype)
    for move in moves:
        move.wait()


def join(table, tail, head):
    more = 2 * BAND * 2 * WIDTH
    return pl.pallas_call(
        join_kernel,
        out_shape=jax.ShapeDtypeStruct((table.shape[0] + more,) + table.shape[1:], table.dtype),
        in_specs=[ANY] * 5,
        out_specs=VMEM,
        scratch_shapes=[pltpu.SemaphoreType.DMA((5,))],
        name="join",
        **settings(12),
    )(table, *tail, *head)


def plan_kernel(half, owner, sizes, place, c_offsets, own, other, out, raw, spots, sem):
    moves = [
        pltpu.make_async_copy(ref.at[pl.ds(ref.shape[0] - 16, 16)], raw.at[h], sem.at[h])
        for h, ref in enumerate((own, other))
    ]
    for move in moves:
        move.start()
    atoms = c_offsets.shape[0]
    slots = c_offsets.shape[1] // 2
    start, layer, me = place[0], place[1], place[2]
    width = slots * atoms
    iota = lambda dim: lax.broadcasted_iota(jnp.int32, (atoms, width), dim)
    spread = (lax.rem(iota(1), atoms) == iota(0)).astype(jnp.float32)
    pick = lax.broadcasted_iota(jnp.int32, (2 * slots, width), 0)
    slot = lax.broadcasted_iota(jnp.int32, (2 * slots, width), 1) // atoms + layer * slots
    dot = functools.partial(jnp.dot, preferred_element_type=jnp.float32)
    aim = dot(c_offsets[...].astype(jnp.float32), (pick == slot).astype(jnp.float32))
    aim = dot(jnp.ones((2 * half, atoms), jnp.float32), aim * spread)
    for move in moves:
        move.wait()
    shift = [raw[h].astype(jnp.float32)[:half, :atoms] for h in range(2)]
    shift = dot(jnp.concatenate(shift, axis=0), spread)
    shift, aim = shift.astype(jnp.int32), aim.astype(jnp.int32)
    atom = lax.rem(lax.broadcasted_iota(jnp.int32, (2 * half, width), 1), atoms)
    w = aim - shift + BAND
    spots[:, :width] = jnp.where((w >= 0) & (w < WIDTH), (atom + BAND + shift) * WIDTH + w, -1)
    move = pltpu.make_async_copy(spots, out, sem.at[0])
    move.start()
    move.wait()
    for p in range(atoms):
        out[0, width + p] = sizes[start + p]
    out[1, width] = (owner[0] == me).astype(jnp.int32)


def make_plan(owner, sizes, place, c_offsets, half, own, other):
    return pl.pallas_call(
        functools.partial(plan_kernel, half),
        out_shape=jax.ShapeDtypeStruct((2 * half, 128), jnp.int32),
        in_specs=[SMEM] * 3 + [VMEM, ANY, ANY],
        out_specs=SMEM,
        scratch_shapes=[
            pltpu.VMEM((2, 16, 128), jnp.bfloat16),
            pltpu.VMEM((2 * half, 128), jnp.int32),
            pltpu.SemaphoreType.DMA((2,)),
        ],
        name="plan",
        **settings(4),
    )(owner, sizes, place, c_offsets, own, other)


def product_kernel(cfg, plan, *refs):
    refs = list(refs)
    near = refs[: cfg["n_near"]]
    del refs[: cfg["n_near"]]
    far = [refs[2 * i : 2 * i + 2] for i in range(cfg["n_far"])]
    del refs[: 2 * cfg["n_far"]]
    table = refs.pop(0)
    out, a_v, o_v, a_sem, o_sem = refs[cfg["aliased"] :]
    chosen, row0, atoms = cfg["chosen"], cfg["row0"], cfg["atoms"]
    count, slots, tile, _ = o_v.shape
    height = a_v.shape[1] // count
    half = height // tile

    def fetch(pieces):
        moves, at = [], 0
        for pair in pieces:
            n = pair[0].shape[0] // height * height
            for h in range(2):
                move = pltpu.make_async_copy(
                    pair[h].at[pl.ds(0, n)], a_v.at[h, pl.ds(at, n)], a_sem.at[len(moves)]
                )
                moves.append(move)
            at += n
        for move in moves:
            move.start()
        for move in moves:
            move.wait()

    if near:
        mine = plan[1, slots * atoms]
        pl.when(mine == 1)(lambda: fetch([near]))
        pl.when(mine != 1)(lambda: fetch(far))
    else:
        fetch(far)
    zero_at = table.shape[0] // 2 - 1
    row_iota = lax.broadcasted_iota(jnp.int32, (tile, 2 * tile), 0)
    first = [p == chosen[0] + n for n, p in enumerate(chosen)].count(True)
    jump = chosen[-1] - chosen[0] + 1 - count

    def one_atom(n, _):
        p = chosen[0] + n + jnp.where(n < first, 0, jump)

        def factor(t, s):
            at = plan[t, s * atoms + p]
            at = 2 * jnp.where(at < 0, zero_at, at - row0 * WIDTH)
            return jnp.concatenate([table[at], table[at + 1]], axis=0)

        size = plan[0, slots * atoms + p]
        for q in range(slots // 2):
            total = jnp.zeros((tile, 2 * tile), jnp.float32)
            for t in range(2 * half):
                left = a_v[t // half, pl.ds(n * height + t % half * tile, tile)]
                left = jnp.concatenate([left, left], axis=1)
                right = jnp.concatenate([factor(t, 2 * q), factor(t, 2 * q + 1)], axis=1)
                total += jnp.dot(left, right, preferred_element_type=jnp.float32)
            total = jnp.where(row_iota < size, total, 0.0).astype(jnp.bfloat16)
            o_v[n, 2 * q] = total[:, :tile]
            o_v[n, 2 * q + 1] = total[:, tile:]
        pltpu.make_async_copy(o_v.at[n], out.at[p], o_sem.at[n]).start()
        return 0

    lax.fori_loop(0, count, one_atom, 0)
    for n, p in enumerate(chosen):
        pltpu.make_async_copy(o_v.at[n], out.at[p], o_sem.at[n]).wait()


def products(plan, far, table, row0, chosen, slots, atoms, half, near=(), prior=None):
    tile = table.shape[-1]
    count = len(chosen)
    operands = [plan, *near, *[f for pair in far for f in pair], table]
    specs = [SMEM] + [ANY] * (len(operands) - 2) + [VMEM]
    aliases = {}
    if prior is not None:
        aliases = {len(operands): 0}
        operands.append(prior)
        specs.append(ANY)
    cfg = dict(
        atoms=atoms,
        chosen=chosen,
        row0=row0,
        n_near=len(near),
        n_far=len(far),
        aliased=len(aliases),
    )
    return pl.pallas_call(
        functools.partial(product_kernel, cfg),
        out_shape=jax.ShapeDtypeStruct((atoms, slots, tile, tile), jnp.bfloat16),
        in_specs=specs,
        out_specs=ANY,
        scratch_shapes=[
            pltpu.VMEM((2, count * half * tile, tile), jnp.bfloat16),
            pltpu.VMEM((count, slots, tile, tile), jnp.bfloat16),
            pltpu.SemaphoreType.DMA((2 * len(far),)),
            pltpu.SemaphoreType.DMA((count,)),
        ],
        input_output_aliases=aliases,
        name="products",
        **settings(12),
    )(*operands)


def after(x, *others):
    return lax.optimization_barrier((x,) + others)[0]


def local(a_tiles, a_offsets, atom_owner, b_tiles, b_offsets, c_offsets, block_sizes):
    cols = lax.axis_size("col")
    cycle = lax.axis_size("row") * cols
    atoms = atom_owner.shape[0]
    bucket = a_tiles.shape[3]
    slots = c_offsets.shape[1] // 2
    me = lax.axis_index("col")
    layer = lax.axis_index("layer")
    start = (lax.axis_index("row") * cols + me) * atoms
    place = jnp.stack([start, layer, me]).astype(jnp.int32)
    assert atoms * cycle > 8 * BAND and lax.axis_size("layer") == 2 and atoms >= 4 * BAND

    def across(x):
        return lax.ppermute(x, "layer", [(0, 1), (1, 0)])

    def swap(x):
        return lax.ppermute(x, "col", [(0, 1), (1, 0)])

    def onward(x):
        return lax.ppermute(x, ("row", "col"), [(i, (i + 1) % cycle) for i in range(cycle)])

    def back(x):
        return lax.ppermute(x, ("row", "col"), [((i + 1) % cycle, i) for i in range(cycle)])

    half, tile = a_tiles.shape[4:6]
    inner = tuple(range(BAND, atoms - BAND))
    outer = tuple(range(BAND)) + tuple(range(atoms - BAND, atoms))
    offsets = jnp.swapaxes(a_offsets, 3, 4)
    a_rows = a_tiles.reshape(a_tiles.shape[:4] + (half * tile, tile))
    whole = cols == 2 and bucket == atoms
    common = dict(slots=slots, atoms=atoms, half=half)
    if whole:
        (sent,) = cut(a_rows, (inner,), 56, offsets=offsets)
        b_offsets = after(b_offsets, sent)
        b_peer = across(b_tiles)
        own_rows = lax.dynamic_slice_in_dim(b_offsets, start, atoms, 0)
        far = swap(sent)
        table, tail, head = band_sums(own_rows, block_sizes, place, b_tiles, b_peer)
        (rest,) = cut(a_rows, (outer,), 8, earlier=(tail,))
        tail, head = onward(tail), back(head)
        rest = swap(rest)
        far = choose(atom_owner, a_rows, offsets, after(far, table), inner)
        far = [(f, across(f)) for f in far]
        plan = make_plan(atom_owner, block_sizes, place, c_offsets, half, *far[-1])
        c = products(plan, far, table, BAND, inner, **common)
        joined = join(table, (tail, across(tail)), (head, across(head)))
        (near,) = cut(a_rows, (outer,), 8, away=False, earlier=(table,))
        near = (near, across(near))
        rest = after(rest, c, joined)
        rest = [(rest, across(rest))]
        return products(plan, rest, joined, 0, outer, near=near, prior=c, **common)
    b_peer = across(b_tiles)
    own_rows = lax.dynamic_slice_in_dim(b_offsets, start, atoms, 0)
    table, tail, head = band_sums(own_rows, block_sizes, place, b_tiles, b_peer)
    tail, head = onward(tail), back(head)
    received = lax.all_to_all(a_tiles, "col", split_axis=2, concat_axis=1, tiled=True)
    moved = lax.all_to_all(a_offsets, "col", split_axis=2, concat_axis=1, tiled=True)
    received = received.reshape((-1,) + received.shape[4:])
    moved = moved.reshape((-1,) + moved.shape[4:])
    places = jnp.arange(atoms, dtype=jnp.int32)
    same = atom_owner[:, None] == atom_owner[None, :]
    rank = jnp.sum(same & (places[None, :] < places[:, None]), axis=1)
    source = atom_owner * bucket + rank
    rows = jnp.take(received, source, axis=0).reshape(-1, tile)
    shift = jnp.take(moved, source, axis=0).T.astype(jnp.bfloat16)
    rows = jnp.concatenate([rows, jnp.pad(shift, ((0, 16 - half), (0, tile - atoms)))], axis=0)
    other = across(rows)
    plan = make_plan(atom_owner, block_sizes, place, c_offsets, half, rows, other)
    cuts = [p * half * tile for p in (0, BAND, atoms - BAND, atoms)]
    low, mid, top = ((rows[i:j], other[i:j]) for i, j in zip(cuts[:-1], cuts[1:], strict=True))
    c = products(plan, [mid], table, BAND, inner, **common)
    table = join(table, (tail, across(tail)), (head, across(head)))
    return products(plan, [low, top], table, 0, outer, prior=c, **common)


def solution(mesh):
    placed = (
        P(("groups", "row"), "col", None, None, "layer", None, None),
        P(("groups", "row"), "col", None, None, "layer"),
        P(("groups", "row", "col")),
        P(("groups", "row", "col"), "layer", None, None),
        P("groups", None),
        P(("groups", "row", "col"), None),
        P("groups"),
    )
    return jax.shard_map(
        local,
        mesh=mesh,
        in_specs=placed,
        out_specs=P(("groups", "row", "col"), "layer", None, None),
        check_vma=False,
    )
```

```python
import functools

import jax
import jax.numpy as jnp
from jax import lax
from jax.experimental import pallas as pl
from jax.experimental.pallas import tpu as pltpu
from jax.sharding import PartitionSpec as P

BAND = 2
WIDTH = 2 * BAND + 1
SMEM = pl.BlockSpec(memory_space=pltpu.SMEM)
VMEM = pl.BlockSpec(memory_space=pltpu.VMEM)
ANY = pl.BlockSpec(memory_space=pl.ANY)


def settings(mib):
    return dict(
        compiler_params=pltpu.CompilerParams(vmem_limit_bytes=mib * 2**20),
        cost_estimate=pl.CostEstimate(flops=1, bytes_accessed=1, transcendentals=0),
    )


def cut_kernel(chosen, away, a_rows, *refs):
    out, held, in_sem, out_sem = refs[-4:]
    height = a_rows.shape[4]
    me = lax.axis_index("col")
    d = 1 - me if away else me
    moves = [
        pltpu.make_async_copy(
            a_rows.at[0, 0, d, p], held.at[pl.ds(j * height, height)], in_sem.at[j]
        )
        for j, p in enumerate(chosen)
    ]
    for move in moves:
        move.start()
    for move in moves:
        move.wait()
    back = pltpu.make_async_copy(held, out, out_sem)
    back.start()
    back.wait()


def cut(a_rows, chosen, earlier, away=True):
    shape = jax.ShapeDtypeStruct((len(chosen) * a_rows.shape[4], a_rows.shape[5]), a_rows.dtype)
    return pl.pallas_call(
        functools.partial(cut_kernel, chosen, away),
        out_shape=shape,
        in_specs=[ANY, ANY],
        out_specs=ANY,
        scratch_shapes=[
            pltpu.VMEM(shape.shape, shape.dtype),
            pltpu.SemaphoreType.DMA((len(chosen),)),
            pltpu.SemaphoreType.DMA,
        ],
        name="cut",
        **settings(8),
    )(a_rows, earlier)


def choose_kernel(chosen, owner, a_rows, offsets, far, tail, head, first, second, raw, sem):
    height, tile = a_rows.shape[4:]
    me = lax.axis_index("col")
    mine = owner[0] == me
    split = first.shape[0] // height
    count = len(chosen)

    def run(here):
        if here:
            pairs = []
            for i, p in enumerate(chosen):
                out, at = (first, i) if i < split else (second, i - split)
                pairs.append((a_rows.at[0, 0, me, p], out.at[pl.ds(at * height, height)]))
        else:
            n = (count - split) * height
            pairs = [
                (far.at[pl.ds(0, split * height)], first),
                (far.at[pl.ds(split * height, n)], second.at[pl.ds(0, n)]),
            ]
        moves = [pltpu.make_async_copy(*p, sem.at[i]) for i, p in enumerate(pairs)]
        for move in moves:
            move.start()
        if here:
            half, atoms = offsets.shape[3:]
            move = pltpu.make_async_copy(offsets.at[0, 0, me], raw, sem.at[count])
            move.start()
            move.wait()
            values = jnp.pad(raw[...].astype(jnp.float32), ((0, 16 - half), (0, tile - atoms)))
            second[pl.ds((count - split) * height, 16)] = values.astype(second.dtype)
        else:
            def ends(ref):
                src = ref.at[pl.ds(ref.shape[0] - 16, 16)]
                dst = second.at[pl.ds((count - split) * height, 16)]
                move = pltpu.make_async_copy(src, dst, sem.at[count])
                move.start()
                move.wait()

            pl.when(me == 0)(lambda: ends(head))
            pl.when(me != 0)(lambda: ends(tail))
        for move in moves:
            move.wait()

    pl.when(mine)(lambda: run(True))
    pl.when(jnp.logical_not(mine))(lambda: run(False))


def choose(owner, a_rows, offsets, far, tail, head, chosen):
    height, tile = a_rows.shape[4:]
    one = len(chosen) // 2 * height
    shape = lambda n: jax.ShapeDtypeStruct((n, tile), a_rows.dtype)
    return pl.pallas_call(
        functools.partial(choose_kernel, chosen),
        out_shape=(shape(one), shape(far.shape[0] - one + 16)),
        in_specs=[SMEM] + [ANY] * 5,
        out_specs=(VMEM, VMEM),
        scratch_shapes=[
            pltpu.VMEM(offsets.shape[3:], jnp.int32),
            pltpu.SemaphoreType.DMA((len(chosen) + 1,)),
        ],
        name="choose",
        **settings(8),
    )(owner, a_rows, offsets, far, tail, head)


def band_kernel(b_offsets, sizes, place, offsets, b_own, b_peer, table, tail, head, total):
    atoms, half, tile, _ = b_own.shape
    blocks = sizes.shape[0]
    start, layer = place[0], place[1]
    row_iota = lax.broadcasted_iota(jnp.int32, (tile, tile), 0)
    col_iota = lax.broadcasted_iota(jnp.int32, (tile, tile), 1)

    def one_row(k, _):
        for w in range(WIDTH):
            total[w] = jnp.zeros((tile, tile), jnp.float32)
        for part, ref in ((layer, b_own), (1 - layer, b_peer)):
            for j in range(half):
                w = b_offsets[k, part * half + j] + BAND
                total[w] = total[w] + ref[k, j].astype(jnp.float32)
        rows = sizes[start + k]
        for w in range(WIDTH):
            cols = sizes[lax.rem(start + k + w + blocks - BAND, blocks)]
            value = jnp.where((row_iota < rows) & (col_iota < cols), total[w], 0.0)
            high = value.astype(jnp.bfloat16)
            at = 2 * tile * (k * WIDTH + w)
            table[pl.ds(at, tile)] = high
            table[pl.ds(at + tile, tile)] = (value - high.astype(jnp.float32)).astype(jnp.bfloat16)
        return 0

    lax.fori_loop(0, atoms, one_row, 0)
    height = 2 * WIDTH * tile
    table[pl.ds(atoms * height, 2 * tile)] = jnp.zeros((2 * tile, tile), table.dtype)
    places = offsets.shape[3:]
    there = 1 - place[2] if offsets.shape[2] == 2 else 0
    values = offsets[0, 0, pl.ds(there, 1)].reshape(places).astype(jnp.float32)
    values = jnp.pad(values, ((0, 16 - places[0]), (0, tile - places[1]))).astype(jnp.bfloat16)
    for out, row in ((tail, atoms - BAND + layer), (head, layer)):
        out[pl.ds(0, height)] = table[pl.ds(row * height, height)]
        out[pl.ds(height, 16)] = values


def band_sums(b_offsets, sizes, place, offsets, b_own, b_peer):
    atoms, half, tile, _ = b_own.shape
    shape = lambda *dims: jax.ShapeDtypeStruct(dims + (tile,), jnp.bfloat16)
    row = shape(2 * WIDTH * tile + 16)
    return pl.pallas_call(
        band_kernel,
        out_shape=(shape(2 * (atoms * WIDTH + 1) * tile), row, row),
        in_specs=[SMEM, SMEM, SMEM, VMEM, VMEM, VMEM],
        out_specs=(VMEM, VMEM, VMEM),
        scratch_shapes=[pltpu.VMEM((WIDTH, tile, tile), jnp.float32)],
        name="band_sums",
        **settings(16),
    )(b_offsets, sizes, place, offsets, b_own, b_peer)


def join_kernel(table, tail, other_tail, head, other_head, out, sem):
    layer = lax.axis_index("layer")
    tile = table.shape[-1]
    height = 2 * WIDTH * tile
    rows = table.shape[0] // height
    parts = (
        (table, BAND, rows),
        (tail, layer, 1),
        (other_tail, 1 - layer, 1),
        (head, BAND + rows + layer, 1),
        (other_head, BAND + rows + 1 - layer, 1),
    )
    moves = [
        pltpu.make_async_copy(
            src.at[pl.ds(0, n * height)], out.at[pl.ds(at * height, n * height)], sem.at[i]
        )
        for i, (src, at, n) in enumerate(parts)
    ]
    for move in moves:
        move.start()
    out[pl.ds((rows + 2 * BAND) * height, 2 * tile)] = jnp.zeros((2 * tile, tile), out.dtype)
    for move in moves:
        move.wait()


def join(table, tail, head):
    more = 2 * BAND * 2 * WIDTH * table.shape[1]
    return pl.pallas_call(
        join_kernel,
        out_shape=jax.ShapeDtypeStruct((table.shape[0] + more, table.shape[1]), table.dtype),
        in_specs=[ANY] * 5,
        out_specs=VMEM,
        scratch_shapes=[pltpu.SemaphoreType.DMA((5,))],
        name="join",
        **settings(12),
    )(table, *tail, *head)


def plan_kernel(half, owner, sizes, place, c_offsets, own, other, out, raw, spots, sem):
    moves = [
        pltpu.make_async_copy(ref.at[pl.ds(ref.shape[0] - 16, 16)], raw.at[h], sem.at[h])
        for h, ref in enumerate((own, other))
    ]
    for move in moves:
        move.start()
    atoms = c_offsets.shape[0]
    slots = c_offsets.shape[1] // 2
    start, layer, me = place[0], place[1], place[2]
    width = slots * atoms
    iota = lambda dim: lax.broadcasted_iota(jnp.int32, (atoms, width), dim)
    spread = (lax.rem(iota(1), atoms) == iota(0)).astype(jnp.float32)
    pick = lax.broadcasted_iota(jnp.int32, (2 * slots, width), 0)
    slot = lax.broadcasted_iota(jnp.int32, (2 * slots, width), 1) // atoms + layer * slots
    dot = functools.partial(jnp.dot, preferred_element_type=jnp.float32)
    aim = dot(c_offsets[...].astype(jnp.float32), (pick == slot).astype(jnp.float32))
    aim = dot(jnp.ones((2 * half, atoms), jnp.float32), aim * spread)
    for move in moves:
        move.wait()
    shift = [raw[h].astype(jnp.float32)[:half, :atoms] for h in range(2)]
    shift = dot(jnp.concatenate(shift, axis=0), spread)
    shift, aim = shift.astype(jnp.int32), aim.astype(jnp.int32)
    atom = lax.rem(lax.broadcasted_iota(jnp.int32, (2 * half, width), 1), atoms)
    w = aim - shift + BAND
    spots[:, :width] = jnp.where((w >= 0) & (w < WIDTH), (atom + BAND + shift) * WIDTH + w, -1)
    move = pltpu.make_async_copy(spots, out, sem.at[0])
    move.start()
    move.wait()
    for p in range(atoms):
        out[0, width + p] = sizes[start + p]
    out[1, width] = (owner[0] == me).astype(jnp.int32)


def make_plan(owner, sizes, place, c_offsets, half, own, other):
    return pl.pallas_call(
        functools.partial(plan_kernel, half),
        out_shape=jax.ShapeDtypeStruct((2 * half, 128), jnp.int32),
        in_specs=[SMEM] * 3 + [VMEM, ANY, ANY],
        out_specs=SMEM,
        scratch_shapes=[
            pltpu.VMEM((2, 16, 128), jnp.bfloat16),
            pltpu.VMEM((2 * half, 128), jnp.int32),
            pltpu.SemaphoreType.DMA((2,)),
        ],
        name="plan",
        **settings(4),
    )(owner, sizes, place, c_offsets, own, other)


def product_kernel(cfg, plan, *refs):
    refs = list(refs)
    near = refs[: cfg["n_near"]]
    del refs[: cfg["n_near"]]
    far = [refs[2 * i : 2 * i + 2] for i in range(cfg["n_far"])]
    del refs[: 2 * cfg["n_far"]]
    table = refs.pop(0)
    out, o_v, o_sem = refs[cfg["aliased"] :]
    chosen, row0, atoms = cfg["chosen"], cfg["row0"], cfg["atoms"]
    count, slots, tile, _ = o_v.shape
    height = cfg["height"]
    half = height // tile
    zero_at = table.shape[0] // (2 * tile) - 1
    row_iota = lax.broadcasted_iota(jnp.int32, (tile, 2 * tile), 0)

    def run(pair, part):
        for n, p in enumerate(part):
            slot = chosen.index(p)

            def factor(t, s, p=p):
                at = plan[t, s * atoms + p]
                at = 2 * tile * jnp.where(at < 0, zero_at, at - row0 * WIDTH)
                return table[pl.ds(pl.multiple_of(at, 2 * tile), 2 * tile)]

            size = plan[0, slots * atoms + p]
            for q in range(slots // 2):
                total = jnp.zeros((tile, 2 * tile), jnp.float32)
                for t in range(2 * half):
                    left = pair[t // half][pl.ds(n * height + t % half * tile, tile)]
                    left = jnp.concatenate([left, left], axis=1)
                    right = jnp.concatenate([factor(t, 2 * q), factor(t, 2 * q + 1)], axis=1)
                    total += jnp.dot(left, right, preferred_element_type=jnp.float32)
                total = jnp.where(row_iota < size, total, 0.0).astype(jnp.bfloat16)
                o_v[slot, 2 * q] = total[:, :tile]
                o_v[slot, 2 * q + 1] = total[:, tile:]
            pltpu.make_async_copy(o_v.at[slot], out.at[p], o_sem.at[slot]).start()

    def run_far():
        at = 0
        for pair in far:
            n = pair[0].shape[0] // height
            run(pair, chosen[at : at + n])
            at += n

    if near:
        mine = plan[1, slots * atoms]
        pl.when(mine == 1)(lambda: run(near, chosen))
        pl.when(mine != 1)(run_far)
    else:
        run_far()
    for n, p in enumerate(chosen):
        pltpu.make_async_copy(o_v.at[n], out.at[p], o_sem.at[n]).wait()


def products(plan, far, table, row0, chosen, slots, atoms, half, near=(), prior=None):
    tile = table.shape[-1]
    count = len(chosen)
    operands = [plan, *near, *[f for pair in far for f in pair], table]
    specs = [SMEM] + [VMEM] * (len(operands) - 1)
    aliases = {}
    if prior is not None:
        aliases = {len(operands): 0}
        operands.append(prior)
        specs.append(ANY)
    cfg = dict(
        atoms=atoms,
        chosen=chosen,
        row0=row0,
        height=half * tile,
        n_near=len(near),
        n_far=len(far),
        aliased=len(aliases),
    )
    return pl.pallas_call(
        functools.partial(product_kernel, cfg),
        out_shape=jax.ShapeDtypeStruct((atoms, slots, tile, tile), jnp.bfloat16),
        in_specs=specs,
        out_specs=ANY,
        scratch_shapes=[
            pltpu.VMEM((count, slots, tile, tile), jnp.bfloat16),
            pltpu.SemaphoreType.DMA((count,)),
        ],
        input_output_aliases=aliases,
        name="products",
        **settings(12),
    )(*operands)


def after(x, *others):
    return lax.optimization_barrier((x,) + others)[0]


def local(a_tiles, a_offsets, atom_owner, b_tiles, b_offsets, c_offsets, block_sizes):
    cols = lax.axis_size("col")
    cycle = lax.axis_size("row") * cols
    atoms = atom_owner.shape[0]
    bucket = a_tiles.shape[3]
    slots = c_offsets.shape[1] // 2
    me = lax.axis_index("col")
    layer = lax.axis_index("layer")
    start = (lax.axis_index("row") * cols + me) * atoms
    place = jnp.stack([start, layer, me]).astype(jnp.int32)
    assert atoms * cycle > 8 * BAND and lax.axis_size("layer") == 2 and atoms >= 4 * BAND

    def across(x):
        return lax.ppermute(x, "layer", [(0, 1), (1, 0)])

    def swap(x):
        return lax.ppermute(x, "col", [(0, 1), (1, 0)])

    def onward(x):
        return lax.ppermute(x, ("row", "col"), [(i, (i + 1) % cycle) for i in range(cycle)])

    def back(x):
        return lax.ppermute(x, ("row", "col"), [((i + 1) % cycle, i) for i in range(cycle)])

    half, tile = a_tiles.shape[4:6]
    inner = tuple(range(BAND, atoms - BAND))
    outer = tuple(range(BAND)) + tuple(range(atoms - BAND, atoms))
    offsets = jnp.swapaxes(a_offsets, 3, 4)
    a_rows = a_tiles.reshape(a_tiles.shape[:4] + (half * tile, tile))
    whole = cols == 2 and bucket == atoms
    common = dict(slots=slots, atoms=atoms, half=half)
    if whole:
        at = (0, 0, 1 - me, BAND, 0, 0)
        sent = lax.dynamic_slice(a_rows, at, (1, 1, 1, len(inner)) + a_rows.shape[4:])
        sent = sent.reshape(-1, tile)
        b_offsets = after(b_offsets, sent)
        b_peer = across(b_tiles)
        own_rows = lax.dynamic_slice_in_dim(b_offsets, start, atoms, 0)
        far = swap(sent)
        table, tail, head = band_sums(own_rows, block_sizes, place, offsets, b_tiles, b_peer)
        rest = cut(a_rows, outer, tail)
        tail, head = onward(tail), back(head)
        rest = swap(rest)
        far = choose(atom_owner, a_rows, offsets, after(far, table), tail, head, inner)
        far = [(f, across(f)) for f in far]
        plan = make_plan(atom_owner, block_sizes, place, c_offsets, half, *far[-1])
        c = products(plan, far, table, BAND, inner, **common)
        joined = join(table, (tail, across(tail)), (head, across(head)))
        near = cut(a_rows, outer, table, away=False)
        near = (near, across(near))
        rest = after(rest, c, joined)
        rest = [(rest, across(rest))]
        return products(plan, rest, joined, 0, outer, near=near, prior=c, **common)
    b_peer = across(b_tiles)
    own_rows = lax.dynamic_slice_in_dim(b_offsets, start, atoms, 0)
    table, tail, head = band_sums(own_rows, block_sizes, place, offsets, b_tiles, b_peer)
    tail, head = onward(tail), back(head)
    received = lax.all_to_all(a_tiles, "col", split_axis=2, concat_axis=1, tiled=True)
    moved = lax.all_to_all(a_offsets, "col", split_axis=2, concat_axis=1, tiled=True)
    received = received.reshape((-1,) + received.shape[4:])
    moved = moved.reshape((-1,) + moved.shape[4:])
    places = jnp.arange(atoms, dtype=jnp.int32)
    same = atom_owner[:, None] == atom_owner[None, :]
    rank = jnp.sum(same & (places[None, :] < places[:, None]), axis=1)
    source = atom_owner * bucket + rank
    rows = jnp.take(received, source, axis=0).reshape(-1, tile)
    shift = jnp.take(moved, source, axis=0).T.astype(jnp.bfloat16)
    rows = jnp.concatenate([rows, jnp.pad(shift, ((0, 16 - half), (0, tile - atoms)))], axis=0)
    other = across(rows)
    plan = make_plan(atom_owner, block_sizes, place, c_offsets, half, rows, other)
    cuts = [p * half * tile for p in (0, BAND, atoms - BAND, atoms)]
    low, mid, top = ((rows[i:j], other[i:j]) for i, j in zip(cuts[:-1], cuts[1:], strict=True))
    c = products(plan, [mid], table, BAND, inner, **common)
    table = join(table, (tail, across(tail)), (head, across(head)))
    return products(plan, [low, top], table, 0, outer, prior=c, **common)


def solution(mesh):
    placed = (
        P(("groups", "row"), "col", None, None, "layer", None, None),
        P(("groups", "row"), "col", None, None, "layer"),
        P(("groups", "row", "col")),
        P(("groups", "row", "col"), "layer", None, None),
        P("groups", None),
        P(("groups", "row", "col"), None),
        P("groups"),
    )
    return jax.shard_map(
        local,
        mesh=mesh,
        in_specs=placed,
        out_specs=P(("groups", "row", "col"), "layer", None, None),
        check_vma=False,
    )
```

```python
import functools

import jax
import jax.numpy as jnp
from jax import lax
from jax.experimental import pallas as pl
from jax.experimental.pallas import tpu as pltpu
from jax.sharding import PartitionSpec as P

BAND = 2
WIDTH = 2 * BAND + 1
SMEM = pl.BlockSpec(memory_space=pltpu.SMEM)
VMEM = pl.BlockSpec(memory_space=pltpu.VMEM)
ANY = pl.BlockSpec(memory_space=pl.ANY)


def settings(mib):
    return dict(
        compiler_params=pltpu.CompilerParams(vmem_limit_bytes=mib * 2**20),
        cost_estimate=pl.CostEstimate(flops=1, bytes_accessed=1, transcendentals=0),
    )


def cut_kernel(chosen, away, a_rows, *refs):
    out, held, in_sem, out_sem = refs[-4:]
    height = a_rows.shape[4]
    me = lax.axis_index("col")
    d = 1 - me if away else me
    moves = [
        pltpu.make_async_copy(
            a_rows.at[0, 0, d, p], held.at[pl.ds(j * height, height)], in_sem.at[j]
        )
        for j, p in enumerate(chosen)
    ]
    for move in moves:
        move.start()
    for move in moves:
        move.wait()
    back = pltpu.make_async_copy(held, out, out_sem)
    back.start()
    back.wait()


def cut(a_rows, chosen, earlier, away=True):
    shape = jax.ShapeDtypeStruct((len(chosen) * a_rows.shape[4], a_rows.shape[5]), a_rows.dtype)
    return pl.pallas_call(
        functools.partial(cut_kernel, chosen, away),
        out_shape=shape,
        in_specs=[ANY, ANY],
        out_specs=ANY,
        scratch_shapes=[
            pltpu.VMEM(shape.shape, shape.dtype),
            pltpu.SemaphoreType.DMA((len(chosen),)),
            pltpu.SemaphoreType.DMA,
        ],
        name="cut",
        **settings(8),
    )(a_rows, earlier)


def choose_kernel(chosen, owner, a_rows, offsets, far, first, second, raw, sem):
    height, tile = a_rows.shape[4:]
    me = lax.axis_index("col")
    mine = owner[0] == me
    count = len(chosen)
    split, end = first.shape[0], count * height
    rest = end - split
    move = pltpu.make_async_copy(offsets.at[0, 0, me], raw, sem.at[count + 1])
    move.start()

    def run(here):
        if here:
            pairs = []
            for i, p in enumerate(chosen):
                low, high = i * height, (i + 1) * height
                middle = min(max(split, low), high)
                for out, base, i0, i1 in ((first, 0, low, middle), (second, split, middle, high)):
                    if i0 < i1:
                        src = a_rows.at[0, 0, me, p, pl.ds(i0 - low, i1 - i0)]
                        pairs.append((src, out.at[pl.ds(i0 - base, i1 - i0)]))
        else:
            pairs = [
                (far.at[pl.ds(0, split)], first),
                (far.at[pl.ds(split, rest)], second.at[pl.ds(0, rest)]),
            ]
        moves = [pltpu.make_async_copy(*p, sem.at[i]) for i, p in enumerate(pairs)]
        for m in moves:
            m.start()
        for m in moves:
            m.wait()

    pl.when(mine)(lambda: run(True))
    pl.when(jnp.logical_not(mine))(lambda: run(False))
    move.wait()
    half, atoms = offsets.shape[3:]
    values = jnp.pad(raw[...].astype(jnp.float32), ((0, 16 - half), (0, tile - atoms)))
    second[pl.ds(rest, 16)] = values.astype(second.dtype)


def choose(owner, a_rows, offsets, far, chosen, split):
    tile = a_rows.shape[5]
    shape = lambda n: jax.ShapeDtypeStruct((n, tile), a_rows.dtype)
    return pl.pallas_call(
        functools.partial(choose_kernel, chosen),
        out_shape=(shape(split), shape(far.shape[0] - split + 16)),
        in_specs=[SMEM] + [ANY] * 3,
        out_specs=(VMEM, VMEM),
        scratch_shapes=[
            pltpu.VMEM(offsets.shape[3:], jnp.int32),
            pltpu.SemaphoreType.DMA((len(chosen) + 2,)),
        ],
        name="choose",
        **settings(8),
    )(owner, a_rows, offsets, far)


def band_kernel(b_offsets, sizes, place, offsets, b_own, b_peer, table, tail, head, total):
    atoms, half, tile, _ = b_own.shape
    blocks = sizes.shape[0]
    start, layer = place[0], place[1]
    row_iota = lax.broadcasted_iota(jnp.int32, (tile, tile), 0)
    col_iota = lax.broadcasted_iota(jnp.int32, (tile, tile), 1)

    def one_row(k, _):
        for w in range(WIDTH):
            total[w] = jnp.zeros((tile, tile), jnp.float32)
        for part, ref in ((layer, b_own), (1 - layer, b_peer)):
            for j in range(half):
                w = b_offsets[k, part * half + j] + BAND
                total[w] = total[w] + ref[k, j].astype(jnp.float32)
        rows = sizes[start + k]
        for w in range(WIDTH):
            cols = sizes[lax.rem(start + k + w + blocks - BAND, blocks)]
            value = jnp.where((row_iota < rows) & (col_iota < cols), total[w], 0.0)
            high = value.astype(jnp.bfloat16)
            at = 2 * tile * (k * WIDTH + w)
            table[pl.ds(at, tile)] = high
            table[pl.ds(at + tile, tile)] = (value - high.astype(jnp.float32)).astype(jnp.bfloat16)
        return 0

    lax.fori_loop(0, atoms, one_row, 0)
    height = 2 * WIDTH * tile
    table[pl.ds(atoms * height, 2 * tile)] = jnp.zeros((2 * tile, tile), table.dtype)
    places = offsets.shape[3:]
    there = 1 - place[2] if offsets.shape[2] == 2 else 0
    values = offsets[0, 0, pl.ds(there, 1)].reshape(places).astype(jnp.float32)
    values = jnp.pad(values, ((0, 16 - places[0]), (0, tile - places[1]))).astype(jnp.bfloat16)
    for out, row in ((tail, atoms - BAND + layer), (head, layer)):
        out[pl.ds(0, height)] = table[pl.ds(row * height, height)]
        out[pl.ds(height, 16)] = values


def band_sums(b_offsets, sizes, place, offsets, b_own, b_peer):
    atoms, half, tile, _ = b_own.shape
    shape = lambda *dims: jax.ShapeDtypeStruct(dims + (tile,), jnp.bfloat16)
    row = shape(2 * WIDTH * tile + 16)
    return pl.pallas_call(
        band_kernel,
        out_shape=(shape(2 * (atoms * WIDTH + 1) * tile), row, row),
        in_specs=[SMEM, SMEM, SMEM, VMEM, VMEM, VMEM],
        out_specs=(VMEM, VMEM, VMEM),
        scratch_shapes=[pltpu.VMEM((WIDTH, tile, tile), jnp.float32)],
        name="band_sums",
        **settings(16),
    )(b_offsets, sizes, place, offsets, b_own, b_peer)


def join_kernel(table, tail, other_tail, head, other_head, out, sem):
    layer = lax.axis_index("layer")
    tile = table.shape[-1]
    height = 2 * WIDTH * tile
    rows = table.shape[0] // height
    parts = (
        (table, BAND, rows),
        (tail, layer, 1),
        (other_tail, 1 - layer, 1),
        (head, BAND + rows + layer, 1),
        (other_head, BAND + rows + 1 - layer, 1),
    )
    moves = [
        pltpu.make_async_copy(
            src.at[pl.ds(0, n * height)], out.at[pl.ds(at * height, n * height)], sem.at[i]
        )
        for i, (src, at, n) in enumerate(parts)
    ]
    for move in moves:
        move.start()
    out[pl.ds((rows + 2 * BAND) * height, 2 * tile)] = jnp.zeros((2 * tile, tile), out.dtype)
    for move in moves:
        move.wait()


def join(table, tail, head):
    more = 2 * BAND * 2 * WIDTH * table.shape[1]
    return pl.pallas_call(
        join_kernel,
        out_shape=jax.ShapeDtypeStruct((table.shape[0] + more, table.shape[1]), table.dtype),
        in_specs=[ANY] * 5,
        out_specs=VMEM,
        scratch_shapes=[pltpu.SemaphoreType.DMA((5,))],
        name="join",
        **settings(12),
    )(table, *tail, *head)


def plan_kernel(half, n_src, owner, sizes, place, c_offsets, *refs):
    pairs = [refs[2 * i : 2 * i + 2] for i in range(n_src)]
    out, raw, spots, sem = refs[2 * n_src :]

    def load(pair):
        moves = [
            pltpu.make_async_copy(ref.at[pl.ds(ref.shape[0] - 16, 16)], raw.at[h], sem.at[h])
            for h, ref in enumerate(pair)
        ]
        for move in moves:
            move.start()
        for move in moves:
            move.wait()

    if n_src == 1:
        load(pairs[0])
    else:
        mine = owner[0] == place[2]
        pl.when(mine)(lambda: load(pairs[0]))
        pl.when(jnp.logical_not(mine) & (place[2] == 0))(lambda: load(pairs[1]))
        pl.when(jnp.logical_not(mine) & (place[2] != 0))(lambda: load(pairs[2]))
    atoms = c_offsets.shape[0]
    slots = c_offsets.shape[1] // 2
    start, layer, me = place[0], place[1], place[2]
    width = slots * atoms
    iota = lambda dim: lax.broadcasted_iota(jnp.int32, (atoms, width), dim)
    spread = (lax.rem(iota(1), atoms) == iota(0)).astype(jnp.float32)
    pick = lax.broadcasted_iota(jnp.int32, (2 * slots, width), 0)
    slot = lax.broadcasted_iota(jnp.int32, (2 * slots, width), 1) // atoms + layer * slots
    dot = functools.partial(jnp.dot, preferred_element_type=jnp.float32)
    aim = dot(c_offsets[...].astype(jnp.float32), (pick == slot).astype(jnp.float32))
    aim = dot(jnp.ones((2 * half, atoms), jnp.float32), aim * spread)
    shift = [raw[h].astype(jnp.float32)[:half, :atoms] for h in range(2)]
    shift = dot(jnp.concatenate(shift, axis=0), spread)
    shift, aim = shift.astype(jnp.int32), aim.astype(jnp.int32)
    atom = lax.rem(lax.broadcasted_iota(jnp.int32, (2 * half, width), 1), atoms)
    w = aim - shift + BAND
    spots[:, :width] = jnp.where((w >= 0) & (w < WIDTH), (atom + BAND + shift) * WIDTH + w, -1)
    move = pltpu.make_async_copy(spots, out, sem.at[0])
    move.start()
    move.wait()
    for p in range(atoms):
        out[0, width + p] = sizes[start + p]
    out[1, width] = (owner[0] == me).astype(jnp.int32)


def make_plan(owner, sizes, place, c_offsets, half, *pairs):
    return pl.pallas_call(
        functools.partial(plan_kernel, half, len(pairs)),
        out_shape=jax.ShapeDtypeStruct((2 * half, 128), jnp.int32),
        in_specs=[SMEM] * 3 + [VMEM] + [ANY] * (2 * len(pairs)),
        out_specs=SMEM,
        scratch_shapes=[
            pltpu.VMEM((2, 16, 128), jnp.bfloat16),
            pltpu.VMEM((2 * half, 128), jnp.int32),
            pltpu.SemaphoreType.DMA((2,)),
        ],
        name="plan",
        **settings(4),
    )(owner, sizes, place, c_offsets, *[ref for pair in pairs for ref in pair])


def product_kernel(cfg, plan, *refs):
    refs = list(refs)
    halves = cfg["halves"]
    take = lambda n: [refs.pop(0) for _ in range(n)]
    near = dict(zip(halves, take(cfg["n_near"]), strict=False))
    far = [dict(zip(halves, take(len(halves)), strict=True)) for _ in range(cfg["n_far"])]
    (table,) = take(1)
    begun = take(cfg["begun"])
    take(cfg["aliased"])
    out = refs[0]
    chosen, atoms, half, slots = cfg["chosen"], cfg["atoms"], cfg["half"], cfg["slots"]
    tile = table.shape[-1]
    zero_at = table.shape[0] // (2 * tile) - 1
    row_iota = lax.broadcasted_iota(jnp.int32, (tile, 2 * tile), 0)

    def run(pieces):
        spots = [(p, i) for p in pieces for i in range(p[halves[0]].shape[0] // tile)]
        for n, p in enumerate(chosen):

            def factor(t, s, p=p):
                at = plan[t, s * atoms + p]
                at = 2 * tile * jnp.where(at < 0, zero_at, at)
                return table[pl.ds(pl.multiple_of(at, 2 * tile), 2 * tile)]

            size = plan[0, slots * atoms + p]
            for q in range(slots // 2):
                total = begun[0][n, q] if begun else jnp.zeros((tile, 2 * tile), jnp.float32)
                for t in range(2 * half):
                    if t // half not in halves:
                        continue
                    piece, i = spots[n * half + t % half]
                    left = piece[t // half][pl.ds(i * tile, tile)]
                    left = jnp.concatenate([left, left], axis=1)
                    right = jnp.concatenate([factor(t, 2 * q), factor(t, 2 * q + 1)], axis=1)
                    total += jnp.dot(left, right, preferred_element_type=jnp.float32)
                if cfg["partial"]:
                    out[n, q] = total
                    continue
                total = jnp.where(row_iota < size, total, 0.0).astype(jnp.bfloat16)
                o_v, o_sem = refs[1:]
                o_v[n, 2 * q] = total[:, :tile]
                o_v[n, 2 * q + 1] = total[:, tile:]
            if not cfg["partial"]:
                pltpu.make_async_copy(o_v.at[n], out.at[p], o_sem.at[n]).start()

    if near:
        mine = plan[1, slots * atoms]
        pl.when(mine == 1)(lambda: run([near]))
        pl.when(mine != 1)(lambda: run(far))
    else:
        run(far)
    if not cfg["partial"]:
        o_v, o_sem = refs[1:]
        for n, p in enumerate(chosen):
            pltpu.make_async_copy(o_v.at[n], out.at[p], o_sem.at[n]).wait()


def products(
    plan, far, table, chosen, slots, atoms, half, near=(), prior=None, halves=(0, 1), begun=None, partial=False
):
    tile = table.shape[-1]
    count = len(chosen)
    operands = [plan, *near, *[f for pair in far for f in pair], table]
    operands += [] if begun is None else [begun]
    specs = [SMEM] + [VMEM] * (len(operands) - 1)
    aliases = {}
    if prior is not None:
        aliases = {len(operands): 0}
        operands.append(prior)
        specs.append(ANY)
    cfg = dict(
        atoms=atoms,
        chosen=chosen,
        half=half,
        slots=slots,
        halves=halves,
        n_near=len(near),
        n_far=len(far),
        begun=int(begun is not None),
        partial=partial,
        aliased=len(aliases),
    )
    out_shape = jax.ShapeDtypeStruct((atoms, slots, tile, tile), jnp.bfloat16)
    if partial:
        out_shape = jax.ShapeDtypeStruct((count, slots // 2, tile, 2 * tile), jnp.float32)
    return pl.pallas_call(
        functools.partial(product_kernel, cfg),
        out_shape=out_shape,
        in_specs=specs,
        out_specs=VMEM if partial else ANY,
        scratch_shapes=[]
        if partial
        else [
            pltpu.VMEM((count, slots, tile, tile), jnp.bfloat16),
            pltpu.SemaphoreType.DMA((count,)),
        ],
        input_output_aliases=aliases,
        name="products",
        **settings(12),
    )(*operands)


def after(x, *others):
    return lax.optimization_barrier((x,) + others)[0]


def local(a_tiles, a_offsets, atom_owner, b_tiles, b_offsets, c_offsets, block_sizes):
    cols = lax.axis_size("col")
    cycle = lax.axis_size("row") * cols
    atoms = atom_owner.shape[0]
    bucket = a_tiles.shape[3]
    slots = c_offsets.shape[1] // 2
    me = lax.axis_index("col")
    layer = lax.axis_index("layer")
    start = (lax.axis_index("row") * cols + me) * atoms
    place = jnp.stack([start, layer, me]).astype(jnp.int32)
    assert atoms * cycle > 8 * BAND and lax.axis_size("layer") == 2 and atoms >= 4 * BAND

    def across(x):
        return lax.ppermute(x, "layer", [(0, 1), (1, 0)])

    def swap(x):
        return lax.ppermute(x, "col", [(0, 1), (1, 0)])

    def onward(x):
        return lax.ppermute(x, ("row", "col"), [(i, (i + 1) % cycle) for i in range(cycle)])

    def back(x):
        return lax.ppermute(x, ("row", "col"), [((i + 1) % cycle, i) for i in range(cycle)])

    half, tile = a_tiles.shape[4:6]
    inner = tuple(range(1, atoms - BAND))
    outer = (0,) + tuple(range(atoms - BAND, atoms))
    offsets = jnp.swapaxes(a_offsets, 3, 4)
    a_rows = a_tiles.reshape(a_tiles.shape[:4] + (half * tile, tile))
    whole = cols == 2 and bucket == atoms
    common = dict(slots=slots, atoms=atoms, half=half)
    if whole:
        at = (0, 0, 1 - me, inner[0], 0, 0)
        sent = lax.dynamic_slice(a_rows, at, (1, 1, 1, len(inner)) + a_rows.shape[4:])
        sent = sent.reshape(-1, tile)
        b_offsets = after(b_offsets, sent)
        b_peer = across(b_tiles)
        own_rows = lax.dynamic_slice_in_dim(b_offsets, start, atoms, 0)
        far = swap(sent)
        table, tail, head = band_sums(own_rows, block_sizes, place, offsets, b_tiles, b_peer)
        rest = cut(a_rows, outer, tail)
        tail, head = onward(tail), back(head)
        rest = swap(rest)
        split = (len(inner) * half // 2 + 1) * tile
        far = choose(atom_owner, a_rows, offsets, after(far, table), inner, split)
        far = [(f, across(f)) for f in far]
        tail, head = (tail, across(tail)), (head, across(head))
        plan = make_plan(atom_owner, block_sizes, place, c_offsets, half, far[-1], head, tail)
        table = join(table, tail, head)
        c = products(plan, far, table, inner, **common)
        near = cut(a_rows, outer, own_rows, away=False)
        near = (near, across(near))
        rest = after(rest, c)
        rest = (rest, across(rest))
        common = dict(common, table=table, chosen=outer)
        begun = products(plan, [rest[:1]], near=near[:1], halves=(0,), partial=True, **common)
        common = dict(common, prior=c, begun=begun)
        return products(plan, [rest[1:]], near=near[1:], halves=(1,), **common)
    b_peer = across(b_tiles)
    own_rows = lax.dynamic_slice_in_dim(b_offsets, start, atoms, 0)
    table, tail, head = band_sums(own_rows, block_sizes, place, offsets, b_tiles, b_peer)
    tail, head = onward(tail), back(head)
    received = lax.all_to_all(a_tiles, "col", split_axis=2, concat_axis=1, tiled=True)
    moved = lax.all_to_all(a_offsets, "col", split_axis=2, concat_axis=1, tiled=True)
    received = received.reshape((-1,) + received.shape[4:])
    moved = moved.reshape((-1,) + moved.shape[4:])
    places = jnp.arange(atoms, dtype=jnp.int32)
    same = atom_owner[:, None] == atom_owner[None, :]
    rank = jnp.sum(same & (places[None, :] < places[:, None]), axis=1)
    source = atom_owner * bucket + rank
    rows = jnp.take(received, source, axis=0).reshape(-1, tile)
    shift = jnp.take(moved, source, axis=0).T.astype(jnp.bfloat16)
    rows = jnp.concatenate([rows, jnp.pad(shift, ((0, 16 - half), (0, tile - atoms)))], axis=0)
    other = across(rows)
    plan = make_plan(atom_owner, block_sizes, place, c_offsets, half, (rows, other))
    table = join(table, (tail, across(tail)), (head, across(head)))
    return products(plan, [(rows, other)], table, tuple(range(atoms)), **common)


def solution(mesh):
    placed = (
        P(("groups", "row"), "col", None, None, "layer", None, None),
        P(("groups", "row"), "col", None, None, "layer"),
        P(("groups", "row", "col")),
        P(("groups", "row", "col"), "layer", None, None),
        P("groups", None),
        P(("groups", "row", "col"), None),
        P("groups"),
    )
    return jax.shard_map(
        local,
        mesh=mesh,
        in_specs=placed,
        out_specs=P(("groups", "row", "col"), "layer", None, None),
        check_vma=False,
    )
```

```python
import functools

import jax
import jax.numpy as jnp
from jax import lax
from jax.experimental import pallas as pl
from jax.experimental.pallas import tpu as pltpu
from jax.sharding import PartitionSpec as P

BAND = 2
WIDTH = 2 * BAND + 1
SMEM = pl.BlockSpec(memory_space=pltpu.SMEM)
VMEM = pl.BlockSpec(memory_space=pltpu.VMEM)
ANY = pl.BlockSpec(memory_space=pl.ANY)


def settings(mib):
    return dict(
        compiler_params=pltpu.CompilerParams(vmem_limit_bytes=mib * 2**20),
        cost_estimate=pl.CostEstimate(flops=1, bytes_accessed=1, transcendentals=0),
    )


def cut_kernel(chosen, away, a_rows, *refs):
    out, held, in_sem, out_sem = refs[-4:]
    height = a_rows.shape[4]
    me = lax.axis_index("col")
    d = 1 - me if away else me
    moves = [
        pltpu.make_async_copy(
            a_rows.at[0, 0, d, p], held.at[pl.ds(j * height, height)], in_sem.at[j]
        )
        for j, p in enumerate(chosen)
    ]
    for move in moves:
        move.start()
    for move in moves:
        move.wait()
    back = pltpu.make_async_copy(held, out, out_sem)
    back.start()
    back.wait()


def cut(a_rows, chosen, earlier, away=True):
    shape = jax.ShapeDtypeStruct((len(chosen) * a_rows.shape[4], a_rows.shape[5]), a_rows.dtype)
    return pl.pallas_call(
        functools.partial(cut_kernel, chosen, away),
        out_shape=shape,
        in_specs=[ANY, ANY],
        out_specs=ANY,
        scratch_shapes=[
            pltpu.VMEM(shape.shape, shape.dtype),
            pltpu.SemaphoreType.DMA((len(chosen),)),
            pltpu.SemaphoreType.DMA,
        ],
        name="cut",
        **settings(8),
    )(a_rows, earlier)


def choose_kernel(chosen, owner, a_rows, offsets, far_first, far_second, first, second, raw, sem):
    height, tile = a_rows.shape[4:]
    me = lax.axis_index("col")
    mine = owner[0] == me
    count = len(chosen)
    split, end = first.shape[0], count * height
    rest = end - split
    move = pltpu.make_async_copy(offsets.at[0, 0, me], raw, sem.at[count + 1])
    move.start()

    def run(here):
        if here:
            sources = [(a_rows.at[0, 0, me, p], i * height, height) for i, p in enumerate(chosen)]
        else:
            n = far_first.shape[0]
            sources = [(far_first, 0, n), (far_second, n, end - n)]
        moves = []
        for ref, start, size in sources:
            for out, low, high in ((first, 0, split), (second, split, end)):
                i0, i1 = max(start, low), min(start + size, high)
                if i0 < i1:
                    src, dst = ref.at[pl.ds(i0 - start, i1 - i0)], out.at[pl.ds(i0 - low, i1 - i0)]
                    moves.append(pltpu.make_async_copy(src, dst, sem.at[len(moves)]))
        for m in moves:
            m.start()
        for m in moves:
            m.wait()

    pl.when(mine)(lambda: run(True))
    pl.when(jnp.logical_not(mine))(lambda: run(False))
    move.wait()
    half, atoms = offsets.shape[3:]
    values = jnp.pad(raw[...].astype(jnp.float32), ((0, 16 - half), (0, tile - atoms)))
    second[pl.ds(rest, 16)] = values.astype(second.dtype)


def choose(owner, a_rows, offsets, far, chosen, split):
    height, tile = a_rows.shape[4:]
    shape = lambda n: jax.ShapeDtypeStruct((n, tile), a_rows.dtype)
    return pl.pallas_call(
        functools.partial(choose_kernel, chosen),
        out_shape=(shape(split), shape(len(chosen) * height - split + 16)),
        in_specs=[SMEM] + [ANY] * 4,
        out_specs=(VMEM, VMEM),
        scratch_shapes=[
            pltpu.VMEM(offsets.shape[3:], jnp.int32),
            pltpu.SemaphoreType.DMA((len(chosen) + 2,)),
        ],
        name="choose",
        **settings(8),
    )(owner, a_rows, offsets, *far)


def band_kernel(b_offsets, sizes, place, offsets, b_own, b_peer, table, tail, head, total):
    atoms, half, tile, _ = b_own.shape
    blocks = sizes.shape[0]
    start, layer = place[0], place[1]
    row_iota = lax.broadcasted_iota(jnp.int32, (tile, tile), 0)
    col_iota = lax.broadcasted_iota(jnp.int32, (tile, tile), 1)

    def one_row(k, _):
        for w in range(WIDTH):
            total[w] = jnp.zeros((tile, tile), jnp.float32)
        for part, ref in ((layer, b_own), (1 - layer, b_peer)):
            for j in range(half):
                w = b_offsets[k, part * half + j] + BAND
                total[w] = total[w] + ref[k, j].astype(jnp.float32)
        rows = sizes[start + k]
        for w in range(WIDTH):
            cols = sizes[lax.rem(start + k + w + blocks - BAND, blocks)]
            value = jnp.where((row_iota < rows) & (col_iota < cols), total[w], 0.0)
            high = value.astype(jnp.bfloat16)
            at = 2 * tile * (k * WIDTH + w)
            table[pl.ds(at, tile)] = high
            table[pl.ds(at + tile, tile)] = (value - high.astype(jnp.float32)).astype(jnp.bfloat16)
        return 0

    lax.fori_loop(0, atoms, one_row, 0)
    height = 2 * WIDTH * tile
    table[pl.ds(atoms * height, 2 * tile)] = jnp.zeros((2 * tile, tile), table.dtype)
    places = offsets.shape[3:]
    there = 1 - place[2] if offsets.shape[2] == 2 else 0
    values = offsets[0, 0, pl.ds(there, 1)].reshape(places).astype(jnp.float32)
    values = jnp.pad(values, ((0, 16 - places[0]), (0, tile - places[1]))).astype(jnp.bfloat16)
    for out, row in ((tail, atoms - BAND + layer), (head, layer)):
        out[pl.ds(0, height)] = table[pl.ds(row * height, height)]
        out[pl.ds(height, 16)] = values


def band_sums(b_offsets, sizes, place, offsets, b_own, b_peer):
    atoms, half, tile, _ = b_own.shape
    shape = lambda *dims: jax.ShapeDtypeStruct(dims + (tile,), jnp.bfloat16)
    row = shape(2 * WIDTH * tile + 16)
    return pl.pallas_call(
        band_kernel,
        out_shape=(shape(2 * (atoms * WIDTH + 1) * tile), row, row),
        in_specs=[SMEM, SMEM, SMEM, VMEM, VMEM, VMEM],
        out_specs=(VMEM, VMEM, VMEM),
        scratch_shapes=[pltpu.VMEM((WIDTH, tile, tile), jnp.float32)],
        name="band_sums",
        **settings(16),
    )(b_offsets, sizes, place, offsets, b_own, b_peer)


def join_kernel(table, tail, other_tail, head, other_head, out, sem):
    layer = lax.axis_index("layer")
    tile = table.shape[-1]
    height = 2 * WIDTH * tile
    rows = table.shape[0] // height
    parts = (
        (table, BAND, rows),
        (tail, layer, 1),
        (other_tail, 1 - layer, 1),
        (head, BAND + rows + layer, 1),
        (other_head, BAND + rows + 1 - layer, 1),
    )
    moves = [
        pltpu.make_async_copy(
            src.at[pl.ds(0, n * height)], out.at[pl.ds(at * height, n * height)], sem.at[i]
        )
        for i, (src, at, n) in enumerate(parts)
    ]
    for move in moves:
        move.start()
    out[pl.ds((rows + 2 * BAND) * height, 2 * tile)] = jnp.zeros((2 * tile, tile), out.dtype)
    for move in moves:
        move.wait()


def join(table, tail, head):
    more = 2 * BAND * 2 * WIDTH * table.shape[1]
    return pl.pallas_call(
        join_kernel,
        out_shape=jax.ShapeDtypeStruct((table.shape[0] + more, table.shape[1]), table.dtype),
        in_specs=[ANY] * 5,
        out_specs=VMEM,
        scratch_shapes=[pltpu.SemaphoreType.DMA((5,))],
        name="join",
        **settings(12),
    )(table, *tail, *head)


def plan_kernel(half, n_src, owner, sizes, place, c_offsets, *refs):
    pairs = [refs[2 * i : 2 * i + 2] for i in range(n_src)]
    out, raw, spots, sem = refs[2 * n_src :]

    def load(pair):
        moves = [
            pltpu.make_async_copy(ref.at[pl.ds(ref.shape[0] - 16, 16)], raw.at[h], sem.at[h])
            for h, ref in enumerate(pair)
        ]
        for move in moves:
            move.start()
        for move in moves:
            move.wait()

    if n_src == 1:
        load(pairs[0])
    else:
        mine = owner[0] == place[2]
        pl.when(mine)(lambda: load(pairs[0]))
        pl.when(jnp.logical_not(mine) & (place[2] == 0))(lambda: load(pairs[1]))
        pl.when(jnp.logical_not(mine) & (place[2] != 0))(lambda: load(pairs[2]))
    atoms = c_offsets.shape[0]
    slots = c_offsets.shape[1] // 2
    start, layer, me = place[0], place[1], place[2]
    width = slots * atoms
    iota = lambda dim: lax.broadcasted_iota(jnp.int32, (atoms, width), dim)
    spread = (lax.rem(iota(1), atoms) == iota(0)).astype(jnp.float32)
    pick = lax.broadcasted_iota(jnp.int32, (2 * slots, width), 0)
    slot = lax.broadcasted_iota(jnp.int32, (2 * slots, width), 1) // atoms + layer * slots
    dot = functools.partial(jnp.dot, preferred_element_type=jnp.float32)
    aim = dot(c_offsets[...].astype(jnp.float32), (pick == slot).astype(jnp.float32))
    aim = dot(jnp.ones((2 * half, atoms), jnp.float32), aim * spread)
    shift = [raw[h].astype(jnp.float32)[:half, :atoms] for h in range(2)]
    shift = dot(jnp.concatenate(shift, axis=0), spread)
    shift, aim = shift.astype(jnp.int32), aim.astype(jnp.int32)
    atom = lax.rem(lax.broadcasted_iota(jnp.int32, (2 * half, width), 1), atoms)
    w = aim - shift + BAND
    spots[:, :width] = jnp.where((w >= 0) & (w < WIDTH), (atom + BAND + shift) * WIDTH + w, -1)
    move = pltpu.make_async_copy(spots, out, sem.at[0])
    move.start()
    move.wait()
    for p in range(atoms):
        out[0, width + p] = sizes[start + p]
    out[1, width] = (owner[0] == me).astype(jnp.int32)


def make_plan(owner, sizes, place, c_offsets, half, *pairs):
    return pl.pallas_call(
        functools.partial(plan_kernel, half, len(pairs)),
        out_shape=jax.ShapeDtypeStruct((2 * half, 128), jnp.int32),
        in_specs=[SMEM] * 3 + [VMEM] + [ANY] * (2 * len(pairs)),
        out_specs=SMEM,
        scratch_shapes=[
            pltpu.VMEM((2, 16, 128), jnp.bfloat16),
            pltpu.VMEM((2 * half, 128), jnp.int32),
            pltpu.SemaphoreType.DMA((2,)),
        ],
        name="plan",
        **settings(4),
    )(owner, sizes, place, c_offsets, *[ref for pair in pairs for ref in pair])


def product_kernel(cfg, plan, *refs):
    refs = list(refs)
    halves = cfg["halves"]
    take = lambda n: [refs.pop(0) for _ in range(n)]
    near = dict(zip(halves, take(cfg["n_near"]), strict=False))
    far = [dict(zip(halves, take(len(halves)), strict=True)) for _ in range(cfg["n_far"])]
    (table,) = take(1)
    begun = take(cfg["begun"])
    take(cfg["aliased"])
    out = refs[0]
    chosen, atoms, half, slots = cfg["chosen"], cfg["atoms"], cfg["half"], cfg["slots"]
    tile = table.shape[-1]
    zero_at = table.shape[0] // (2 * tile) - 1
    row_iota = lax.broadcasted_iota(jnp.int32, (tile, 2 * tile), 0)

    def run(pieces):
        spots = [(p, i) for p in pieces for i in range(p[halves[0]].shape[0] // tile)]
        for n, p in enumerate(chosen):

            def factor(t, s, p=p):
                at = plan[t, s * atoms + p]
                at = 2 * tile * jnp.where(at < 0, zero_at, at)
                return table[pl.ds(pl.multiple_of(at, 2 * tile), 2 * tile)]

            size = plan[0, slots * atoms + p]
            for q in range(slots // 2):
                total = begun[0][n, q] if begun else jnp.zeros((tile, 2 * tile), jnp.float32)
                for t in range(2 * half):
                    if t // half not in halves:
                        continue
                    piece, i = spots[n * half + t % half]
                    left = piece[t // half][pl.ds(i * tile, tile)]
                    left = jnp.concatenate([left, left], axis=1)
                    right = jnp.concatenate([factor(t, 2 * q), factor(t, 2 * q + 1)], axis=1)
                    total += jnp.dot(left, right, preferred_element_type=jnp.float32)
                if cfg["partial"]:
                    out[n, q] = total
                    continue
                total = jnp.where(row_iota < size, total, 0.0).astype(jnp.bfloat16)
                o_v, o_sem = refs[1:]
                o_v[n, 2 * q] = total[:, :tile]
                o_v[n, 2 * q + 1] = total[:, tile:]
            if not cfg["partial"]:
                pltpu.make_async_copy(o_v.at[n], out.at[p], o_sem.at[n]).start()

    if near:
        mine = plan[1, slots * atoms]
        pl.when(mine == 1)(lambda: run([near]))
        pl.when(mine != 1)(lambda: run(far))
    else:
        run(far)
    if not cfg["partial"]:
        o_v, o_sem = refs[1:]
        for n, p in enumerate(chosen):
            pltpu.make_async_copy(o_v.at[n], out.at[p], o_sem.at[n]).wait()


def products(
    plan, far, table, chosen, slots, atoms, half, near=(), prior=None, halves=(0, 1), begun=None, partial=False
):
    tile = table.shape[-1]
    count = len(chosen)
    operands = [plan, *near, *[f for pair in far for f in pair], table]
    operands += [] if begun is None else [begun]
    specs = [SMEM] + [VMEM] * (len(operands) - 1)
    aliases = {}
    if prior is not None:
        aliases = {len(operands): 0}
        operands.append(prior)
        specs.append(ANY)
    cfg = dict(
        atoms=atoms,
        chosen=chosen,
        half=half,
        slots=slots,
        halves=halves,
        n_near=len(near),
        n_far=len(far),
        begun=int(begun is not None),
        partial=partial,
        aliased=len(aliases),
    )
    out_shape = jax.ShapeDtypeStruct((atoms, slots, tile, tile), jnp.bfloat16)
    if partial:
        out_shape = jax.ShapeDtypeStruct((count, slots // 2, tile, 2 * tile), jnp.float32)
    return pl.pallas_call(
        functools.partial(product_kernel, cfg),
        out_shape=out_shape,
        in_specs=specs,
        out_specs=VMEM if partial else ANY,
        scratch_shapes=[]
        if partial
        else [
            pltpu.VMEM((count, slots, tile, tile), jnp.bfloat16),
            pltpu.SemaphoreType.DMA((count,)),
        ],
        input_output_aliases=aliases,
        name="products",
        **settings(12),
    )(*operands)


def after(x, *others):
    return lax.optimization_barrier((x,) + others)[0]


def local(a_tiles, a_offsets, atom_owner, b_tiles, b_offsets, c_offsets, block_sizes):
    cols = lax.axis_size("col")
    cycle = lax.axis_size("row") * cols
    atoms = atom_owner.shape[0]
    bucket = a_tiles.shape[3]
    slots = c_offsets.shape[1] // 2
    me = lax.axis_index("col")
    layer = lax.axis_index("layer")
    start = (lax.axis_index("row") * cols + me) * atoms
    place = jnp.stack([start, layer, me]).astype(jnp.int32)
    assert atoms * cycle > 8 * BAND and lax.axis_size("layer") == 2 and atoms >= 4 * BAND

    def across(x):
        return lax.ppermute(x, "layer", [(0, 1), (1, 0)])

    def swap(x):
        return lax.ppermute(x, "col", [(0, 1), (1, 0)])

    def onward(x):
        return lax.ppermute(x, ("row", "col"), [(i, (i + 1) % cycle) for i in range(cycle)])

    def back(x):
        return lax.ppermute(x, ("row", "col"), [((i + 1) % cycle, i) for i in range(cycle)])

    half, tile = a_tiles.shape[4:6]
    inner = tuple(range(1, atoms - BAND))
    outer = (0,) + tuple(range(atoms - BAND, atoms))
    offsets = jnp.swapaxes(a_offsets, 3, 4)
    a_rows = a_tiles.reshape(a_tiles.shape[:4] + (half * tile, tile))
    whole = cols == 2 and bucket == atoms
    common = dict(slots=slots, atoms=atoms, half=half)
    if whole:
        all_rows = a_tiles.reshape(a_tiles.shape[:3] + (-1, tile))
        p0, count = inner[0] * half * tile, len(inner) * half * tile
        cut_at = (count + tile) // 2

        def part(at, n):
            rows = lax.dynamic_slice(all_rows, (0, 0, 1 - me, at, 0), (1, 1, 1, n, tile))
            return rows.reshape(n, tile)

        sent = part(p0, cut_at), part(p0 + cut_at, count - cut_at)
        b_offsets = after(b_offsets, *sent)
        b_peer = across(b_tiles)
        own_rows = lax.dynamic_slice_in_dim(b_offsets, start, atoms, 0)
        far = [swap(x) for x in sent]
        table, tail, head = band_sums(own_rows, block_sizes, place, offsets, b_tiles, b_peer)
        rest = cut(a_rows, outer, tail)
        tail, head = onward(tail), back(head)
        rest = swap(rest)
        split = (len(inner) * half // 2 + 1) * tile
        far = choose(atom_owner, a_rows, offsets, [after(f, table) for f in far], inner, split)
        far = [(f, across(f)) for f in far]
        tail, head = (tail, across(tail)), (head, across(head))
        plan = make_plan(atom_owner, block_sizes, place, c_offsets, half, far[-1], head, tail)
        table = join(table, tail, head)
        c = products(plan, far, table, inner, **common)
        near = cut(a_rows, outer, own_rows, away=False)
        near = (near, across(near))
        rest = after(rest, c)
        rest = (rest, across(rest))
        common = dict(common, table=table, chosen=outer)
        begun = products(plan, [rest[:1]], near=near[:1], halves=(0,), partial=True, **common)
        common = dict(common, prior=c, begun=begun)
        return products(plan, [rest[1:]], near=near[1:], halves=(1,), **common)
    b_peer = across(b_tiles)
    own_rows = lax.dynamic_slice_in_dim(b_offsets, start, atoms, 0)
    table, tail, head = band_sums(own_rows, block_sizes, place, offsets, b_tiles, b_peer)
    tail, head = onward(tail), back(head)
    received = lax.all_to_all(a_tiles, "col", split_axis=2, concat_axis=1, tiled=True)
    moved = lax.all_to_all(a_offsets, "col", split_axis=2, concat_axis=1, tiled=True)
    received = received.reshape((-1,) + received.shape[4:])
    moved = moved.reshape((-1,) + moved.shape[4:])
    places = jnp.arange(atoms, dtype=jnp.int32)
    same = atom_owner[:, None] == atom_owner[None, :]
    rank = jnp.sum(same & (places[None, :] < places[:, None]), axis=1)
    source = atom_owner * bucket + rank
    rows = jnp.take(received, source, axis=0).reshape(-1, tile)
    shift = jnp.take(moved, source, axis=0).T.astype(jnp.bfloat16)
    rows = jnp.concatenate([rows, jnp.pad(shift, ((0, 16 - half), (0, tile - atoms)))], axis=0)
    other = across(rows)
    plan = make_plan(atom_owner, block_sizes, place, c_offsets, half, (rows, other))
    table = join(table, (tail, across(tail)), (head, across(head)))
    return products(plan, [(rows, other)], table, tuple(range(atoms)), **common)


def solution(mesh):
    placed = (
        P(("groups", "row"), "col", None, None, "layer", None, None),
        P(("groups", "row"), "col", None, None, "layer"),
        P(("groups", "row", "col")),
        P(("groups", "row", "col"), "layer", None, None),
        P("groups", None),
        P(("groups", "row", "col"), None),
        P("groups"),
    )
    return jax.shard_map(
        local,
        mesh=mesh,
        in_specs=placed,
        out_specs=P(("groups", "row", "col"), "layer", None, None),
        check_vma=False,
    )
```

```python
import functools

import jax
import jax.numpy as jnp
from jax import lax
from jax.experimental import pallas as pl
from jax.experimental.pallas import tpu as pltpu
from jax.sharding import PartitionSpec as P

BAND = 2
WIDTH = 2 * BAND + 1
SMEM = pl.BlockSpec(memory_space=pltpu.SMEM)
VMEM = pl.BlockSpec(memory_space=pltpu.VMEM)
ANY = pl.BlockSpec(memory_space=pl.ANY)


def settings(mib):
    return dict(
        compiler_params=pltpu.CompilerParams(vmem_limit_bytes=mib * 2**20),
        cost_estimate=pl.CostEstimate(flops=1, bytes_accessed=1, transcendentals=0),
    )


def cut_kernel(chosen, away, a_rows, *refs):
    out, held, in_sem, out_sem = refs[-4:]
    height = a_rows.shape[4]
    me = lax.axis_index("col")
    d = 1 - me if away else me
    moves = [
        pltpu.make_async_copy(
            a_rows.at[0, 0, d, p], held.at[pl.ds(j * height, height)], in_sem.at[j]
        )
        for j, p in enumerate(chosen)
    ]
    for move in moves:
        move.start()
    for move in moves:
        move.wait()
    back = pltpu.make_async_copy(held, out, out_sem)
    back.start()
    back.wait()


def cut(a_rows, chosen, earlier, away=True):
    shape = jax.ShapeDtypeStruct((len(chosen) * a_rows.shape[4], a_rows.shape[5]), a_rows.dtype)
    return pl.pallas_call(
        functools.partial(cut_kernel, chosen, away),
        out_shape=shape,
        in_specs=[ANY, ANY],
        out_specs=ANY,
        scratch_shapes=[
            pltpu.VMEM(shape.shape, shape.dtype),
            pltpu.SemaphoreType.DMA((len(chosen),)),
            pltpu.SemaphoreType.DMA,
        ],
        name="cut",
        **settings(8),
    )(a_rows, earlier)


def choose_kernel(chosen, owner, a_rows, offsets, far_first, far_second, first, second, raw, sem):
    height, tile = a_rows.shape[4:]
    me = lax.axis_index("col")
    mine = owner[0] == me
    count = len(chosen)
    split, end = first.shape[0], count * height
    rest = end - split
    move = pltpu.make_async_copy(offsets.at[0, 0, me], raw, sem.at[count + 1])
    move.start()

    def run(here):
        if here:
            sources = [(a_rows.at[0, 0, me, p], i * height, height) for i, p in enumerate(chosen)]
        else:
            n = far_first.shape[0]
            sources = [(far_first, 0, n), (far_second, n, end - n)]
        moves = []
        for ref, start, size in sources:
            for out, low, high in ((first, 0, split), (second, split, end)):
                i0, i1 = max(start, low), min(start + size, high)
                if i0 < i1:
                    src, dst = ref.at[pl.ds(i0 - start, i1 - i0)], out.at[pl.ds(i0 - low, i1 - i0)]
                    moves.append(pltpu.make_async_copy(src, dst, sem.at[len(moves)]))
        for m in moves:
            m.start()
        for m in moves:
            m.wait()

    pl.when(mine)(lambda: run(True))
    pl.when(jnp.logical_not(mine))(lambda: run(False))
    move.wait()
    half, atoms = offsets.shape[3:]
    values = jnp.pad(raw[...].astype(jnp.float32), ((0, 16 - half), (0, tile - atoms)))
    second[pl.ds(rest, 16)] = values.astype(second.dtype)


def choose(owner, a_rows, offsets, far, chosen, split):
    height, tile = a_rows.shape[4:]
    shape = lambda n: jax.ShapeDtypeStruct((n, tile), a_rows.dtype)
    return pl.pallas_call(
        functools.partial(choose_kernel, chosen),
        out_shape=(shape(split), shape(len(chosen) * height - split + 16)),
        in_specs=[SMEM] + [ANY] * 4,
        out_specs=(VMEM, VMEM),
        scratch_shapes=[
            pltpu.VMEM(offsets.shape[3:], jnp.int32),
            pltpu.SemaphoreType.DMA((len(chosen) + 2,)),
        ],
        name="choose",
        **settings(8),
    )(owner, a_rows, offsets, *far)


def band_kernel(pairwise, b_offsets, sizes, place, offsets, b_own, b_peer, table, first, second, total):
    atoms, half, tile, _ = b_own.shape
    blocks = sizes.shape[0]
    start, layer = place[0], place[1]
    row_iota = lax.broadcasted_iota(jnp.int32, (tile, tile), 0)
    col_iota = lax.broadcasted_iota(jnp.int32, (tile, tile), 1)

    def one_row(k, _):
        for w in range(WIDTH):
            total[w] = jnp.zeros((tile, tile), jnp.float32)
        for part, ref in ((layer, b_own), (1 - layer, b_peer)):
            for j in range(half):
                w = b_offsets[k, part * half + j] + BAND
                total[w] = total[w] + ref[k, j].astype(jnp.float32)
        rows = sizes[start + k]
        for w in range(WIDTH):
            cols = sizes[lax.rem(start + k + w + blocks - BAND, blocks)]
            value = jnp.where((row_iota < rows) & (col_iota < cols), total[w], 0.0)
            high = value.astype(jnp.bfloat16)
            at = 2 * tile * (k * WIDTH + w)
            table[pl.ds(at, tile)] = high
            table[pl.ds(at + tile, tile)] = (value - high.astype(jnp.float32)).astype(jnp.bfloat16)
        return 0

    lax.fori_loop(0, atoms, one_row, 0)
    height = 2 * WIDTH * tile
    table[pl.ds(atoms * height, 2 * tile)] = jnp.zeros((2 * tile, tile), table.dtype)
    places = offsets.shape[3:]
    there = 1 - place[2] if offsets.shape[2] == 2 else 0
    values = offsets[0, 0, pl.ds(there, 1)].reshape(places).astype(jnp.float32)
    values = jnp.pad(values, ((0, 16 - places[0]), (0, tile - places[1]))).astype(jnp.bfloat16)
    rows = atoms - BAND + layer, layer
    if pairwise:
        rows = [jnp.where(place[2] == 0, rows[i], rows[1 - i]) for i in range(2)]
    for out, row in zip((first, second), rows, strict=True):
        out[pl.ds(0, height)] = table[pl.ds(row * height, height)]
        out[pl.ds(height, 16)] = values


def band_sums(b_offsets, sizes, place, offsets, b_own, b_peer, pairwise):
    atoms, half, tile, _ = b_own.shape
    shape = lambda *dims: jax.ShapeDtypeStruct(dims + (tile,), jnp.bfloat16)
    row = shape(2 * WIDTH * tile + 16)
    return pl.pallas_call(
        functools.partial(band_kernel, pairwise),
        out_shape=(shape(2 * (atoms * WIDTH + 1) * tile), row, row),
        in_specs=[SMEM, SMEM, SMEM, VMEM, VMEM, VMEM],
        out_specs=(VMEM, VMEM, VMEM),
        scratch_shapes=[pltpu.VMEM((WIDTH, tile, tile), jnp.float32)],
        name="band_sums",
        **settings(16),
    )(b_offsets, sizes, place, offsets, b_own, b_peer)


def join_kernel(pairwise, table, first, other_first, second, other_second, out, sem):
    layer = lax.axis_index("layer")
    tile = table.shape[-1]
    height = 2 * WIDTH * tile
    rows = table.shape[0] // height
    at = 0, BAND + rows
    if pairwise:
        me = lax.axis_index("col")
        at = [jnp.where(me == 0, at[1 - i], at[i]) for i in range(2)]
    parts = (
        (table, BAND, rows),
        (first, at[0] + layer, 1),
        (other_first, at[0] + 1 - layer, 1),
        (second, at[1] + layer, 1),
        (other_second, at[1] + 1 - layer, 1),
    )
    moves = [
        pltpu.make_async_copy(
            src.at[pl.ds(0, n * height)], out.at[pl.ds(at * height, n * height)], sem.at[i]
        )
        for i, (src, at, n) in enumerate(parts)
    ]
    for move in moves:
        move.start()
    out[pl.ds((rows + 2 * BAND) * height, 2 * tile)] = jnp.zeros((2 * tile, tile), out.dtype)
    for move in moves:
        move.wait()


def join(table, first, second, pairwise):
    more = 2 * BAND * 2 * WIDTH * table.shape[1]
    return pl.pallas_call(
        functools.partial(join_kernel, pairwise),
        out_shape=jax.ShapeDtypeStruct((table.shape[0] + more, table.shape[1]), table.dtype),
        in_specs=[ANY] * 5,
        out_specs=VMEM,
        scratch_shapes=[pltpu.SemaphoreType.DMA((5,))],
        name="join",
        **settings(12),
    )(table, *first, *second)


def plan_kernel(half, n_src, owner, sizes, place, c_offsets, *refs):
    pairs = [refs[2 * i : 2 * i + 2] for i in range(n_src)]
    out, raw, spots, sem = refs[2 * n_src :]

    def load(pair):
        moves = [
            pltpu.make_async_copy(ref.at[pl.ds(ref.shape[0] - 16, 16)], raw.at[h], sem.at[h])
            for h, ref in enumerate(pair)
        ]
        for move in moves:
            move.start()
        for move in moves:
            move.wait()

    if n_src == 1:
        load(pairs[0])
    else:
        mine = owner[0] == place[2]
        pl.when(mine)(lambda: load(pairs[0]))
        pl.when(jnp.logical_not(mine))(lambda: load(pairs[1]))
    atoms = c_offsets.shape[0]
    slots = c_offsets.shape[1] // 2
    start, layer, me = place[0], place[1], place[2]
    width = slots * atoms
    iota = lambda dim: lax.broadcasted_iota(jnp.int32, (atoms, width), dim)
    spread = (lax.rem(iota(1), atoms) == iota(0)).astype(jnp.float32)
    pick = lax.broadcasted_iota(jnp.int32, (2 * slots, width), 0)
    slot = lax.broadcasted_iota(jnp.int32, (2 * slots, width), 1) // atoms + layer * slots
    dot = functools.partial(jnp.dot, preferred_element_type=jnp.float32)
    aim = dot(c_offsets[...].astype(jnp.float32), (pick == slot).astype(jnp.float32))
    aim = dot(jnp.ones((2 * half, atoms), jnp.float32), aim * spread)
    shift = [raw[h].astype(jnp.float32)[:half, :atoms] for h in range(2)]
    shift = dot(jnp.concatenate(shift, axis=0), spread)
    shift, aim = shift.astype(jnp.int32), aim.astype(jnp.int32)
    atom = lax.rem(lax.broadcasted_iota(jnp.int32, (2 * half, width), 1), atoms)
    w = aim - shift + BAND
    spots[:, :width] = jnp.where((w >= 0) & (w < WIDTH), (atom + BAND + shift) * WIDTH + w, -1)
    move = pltpu.make_async_copy(spots, out, sem.at[0])
    move.start()
    move.wait()
    for p in range(atoms):
        out[0, width + p] = sizes[start + p]
    out[1, width] = (owner[0] == me).astype(jnp.int32)


def make_plan(owner, sizes, place, c_offsets, half, *pairs):
    return pl.pallas_call(
        functools.partial(plan_kernel, half, len(pairs)),
        out_shape=jax.ShapeDtypeStruct((2 * half, 128), jnp.int32),
        in_specs=[SMEM] * 3 + [VMEM] + [ANY] * (2 * len(pairs)),
        out_specs=SMEM,
        scratch_shapes=[
            pltpu.VMEM((2, 16, 128), jnp.bfloat16),
            pltpu.VMEM((2 * half, 128), jnp.int32),
            pltpu.SemaphoreType.DMA((2,)),
        ],
        name="plan",
        **settings(4),
    )(owner, sizes, place, c_offsets, *[ref for pair in pairs for ref in pair])


def product_kernel(cfg, plan, *refs):
    refs = list(refs)
    halves = cfg["halves"]
    take = lambda n: [refs.pop(0) for _ in range(n)]
    near = dict(zip(halves, take(cfg["n_near"]), strict=False))
    far = [dict(zip(halves, take(len(halves)), strict=True)) for _ in range(cfg["n_far"])]
    (table,) = take(1)
    begun = take(cfg["begun"])
    take(cfg["aliased"])
    out = refs[0]
    chosen, atoms, half, slots = cfg["chosen"], cfg["atoms"], cfg["half"], cfg["slots"]
    tile = table.shape[-1]
    zero_at = table.shape[0] // (2 * tile) - 1
    row_iota = lax.broadcasted_iota(jnp.int32, (tile, 2 * tile), 0)

    def run(pieces):
        spots = [(p, i) for p in pieces for i in range(p[halves[0]].shape[0] // tile)]
        for n, p in enumerate(chosen):

            def factor(t, s, p=p):
                at = plan[t, s * atoms + p]
                at = 2 * tile * jnp.where(at < 0, zero_at, at)
                return table[pl.ds(pl.multiple_of(at, 2 * tile), 2 * tile)]

            size = plan[0, slots * atoms + p]
            for q in range(slots // 2):
                total = begun[0][n, q] if begun else jnp.zeros((tile, 2 * tile), jnp.float32)
                for t in range(2 * half):
                    if t // half not in halves:
                        continue
                    piece, i = spots[n * half + t % half]
                    left = piece[t // half][pl.ds(i * tile, tile)]
                    left = jnp.concatenate([left, left], axis=1)
                    right = jnp.concatenate([factor(t, 2 * q), factor(t, 2 * q + 1)], axis=1)
                    total += jnp.dot(left, right, preferred_element_type=jnp.float32)
                if cfg["partial"]:
                    out[n, q] = total
                    continue
                total = jnp.where(row_iota < size, total, 0.0).astype(jnp.bfloat16)
                o_v, o_sem = refs[1:]
                o_v[n, 2 * q] = total[:, :tile]
                o_v[n, 2 * q + 1] = total[:, tile:]
            if not cfg["partial"]:
                pltpu.make_async_copy(o_v.at[n], out.at[p], o_sem.at[n]).start()

    if near:
        mine = plan[1, slots * atoms]
        pl.when(mine == 1)(lambda: run([near]))
        pl.when(mine != 1)(lambda: run(far))
    else:
        run(far)
    if not cfg["partial"]:
        o_v, o_sem = refs[1:]
        for n, p in enumerate(chosen):
            pltpu.make_async_copy(o_v.at[n], out.at[p], o_sem.at[n]).wait()


def products(
    plan, far, table, chosen, slots, atoms, half, near=(), prior=None, halves=(0, 1), begun=None, partial=False
):
    tile = table.shape[-1]
    count = len(chosen)
    operands = [plan, *near, *[f for pair in far for f in pair], table]
    operands += [] if begun is None else [begun]
    specs = [SMEM] + [VMEM] * (len(operands) - 1)
    aliases = {}
    if prior is not None:
        aliases = {len(operands): 0}
        operands.append(prior)
        specs.append(ANY)
    cfg = dict(
        atoms=atoms,
        chosen=chosen,
        half=half,
        slots=slots,
        halves=halves,
        n_near=len(near),
        n_far=len(far),
        begun=int(begun is not None),
        partial=partial,
        aliased=len(aliases),
    )
    out_shape = jax.ShapeDtypeStruct((atoms, slots, tile, tile), jnp.bfloat16)
    if partial:
        out_shape = jax.ShapeDtypeStruct((count, slots // 2, tile, 2 * tile), jnp.float32)
    return pl.pallas_call(
        functools.partial(product_kernel, cfg),
        out_shape=out_shape,
        in_specs=specs,
        out_specs=VMEM if partial else ANY,
        scratch_shapes=[]
        if partial
        else [
            pltpu.VMEM((count, slots, tile, tile), jnp.bfloat16),
            pltpu.SemaphoreType.DMA((count,)),
        ],
        input_output_aliases=aliases,
        name="products",
        **settings(12),
    )(*operands)


def after(x, *others):
    return lax.optimization_barrier((x,) + others)[0]


def local(a_tiles, a_offsets, atom_owner, b_tiles, b_offsets, c_offsets, block_sizes):
    cols = lax.axis_size("col")
    cycle = lax.axis_size("row") * cols
    atoms = atom_owner.shape[0]
    bucket = a_tiles.shape[3]
    slots = c_offsets.shape[1] // 2
    me = lax.axis_index("col")
    layer = lax.axis_index("layer")
    start = (lax.axis_index("row") * cols + me) * atoms
    place = jnp.stack([start, layer, me]).astype(jnp.int32)
    assert atoms * cycle > 8 * BAND and lax.axis_size("layer") == 2 and atoms >= 4 * BAND

    def across(x):
        return lax.ppermute(x, "layer", [(0, 1), (1, 0)])

    def swap(x):
        return lax.ppermute(x, "col", [(0, 1), (1, 0)])

    def onward(x):
        return lax.ppermute(x, ("row", "col"), [(i, (i + 1) % cycle) for i in range(cycle)])

    def back(x):
        return lax.ppermute(x, ("row", "col"), [((i + 1) % cycle, i) for i in range(cycle)])

    def diagonal(x):
        there = [(i, (i + 1) % cycle) for i in range(1, cycle, 2)]
        return lax.ppermute(x, ("row", "col"), there + [(j, i) for i, j in there])

    half, tile = a_tiles.shape[4:6]
    inner = tuple(range(1, atoms - BAND))
    outer = (0,) + tuple(range(atoms - BAND, atoms))
    offsets = jnp.swapaxes(a_offsets, 3, 4)
    a_rows = a_tiles.reshape(a_tiles.shape[:4] + (half * tile, tile))
    whole = cols == 2 and bucket == atoms
    common = dict(slots=slots, atoms=atoms, half=half)
    if whole:
        all_rows = a_tiles.reshape(a_tiles.shape[:3] + (-1, tile))
        p0, count = inner[0] * half * tile, len(inner) * half * tile
        cut_at = (count - tile) // 2

        def part(at, n):
            rows = lax.dynamic_slice(all_rows, (0, 0, 1 - me, at, 0), (1, 1, 1, n, tile))
            return rows.reshape(n, tile)

        sent = part(p0, cut_at), part(p0 + cut_at, count - cut_at)
        b_offsets = after(b_offsets, *sent)
        b_peer = across(after(b_tiles, sent[1]))
        own_rows = lax.dynamic_slice_in_dim(b_offsets, start, atoms, 0)
        far = [swap(x) for x in sent]
        table, first, second = band_sums(
            own_rows, block_sizes, place, offsets, b_tiles, b_peer, True
        )
        rest = cut(a_rows, outer, first)
        first, second = swap(first), diagonal(second)
        rest = swap(rest)
        split = (len(inner) * half // 2 + 1) * tile
        far = choose(atom_owner, a_rows, offsets, [after(f, table) for f in far], inner, split)
        far = [(f, across(f)) for f in far]
        first, second = (first, across(first)), (second, across(second))
        plan = make_plan(atom_owner, block_sizes, place, c_offsets, half, far[-1], first)
        table = join(table, first, second, True)
        c = products(plan, far, table, inner, **common)
        near = cut(a_rows, outer, own_rows, away=False)
        near = (near, across(near))
        rest = after(rest, c)
        rest = (rest, across(rest))
        common = dict(common, table=table, chosen=outer)
        begun = products(plan, [rest[:1]], near=near[:1], halves=(0,), partial=True, **common)
        common = dict(common, prior=c, begun=begun)
        return products(plan, [rest[1:]], near=near[1:], halves=(1,), **common)
    b_peer = across(b_tiles)
    own_rows = lax.dynamic_slice_in_dim(b_offsets, start, atoms, 0)
    table, tail, head = band_sums(own_rows, block_sizes, place, offsets, b_tiles, b_peer, False)
    tail, head = onward(tail), back(head)
    received = lax.all_to_all(a_tiles, "col", split_axis=2, concat_axis=1, tiled=True)
    moved = lax.all_to_all(a_offsets, "col", split_axis=2, concat_axis=1, tiled=True)
    received = received.reshape((-1,) + received.shape[4:])
    moved = moved.reshape((-1,) + moved.shape[4:])
    places = jnp.arange(atoms, dtype=jnp.int32)
    same = atom_owner[:, None] == atom_owner[None, :]
    rank = jnp.sum(same & (places[None, :] < places[:, None]), axis=1)
    source = atom_owner * bucket + rank
    rows = jnp.take(received, source, axis=0).reshape(-1, tile)
    shift = jnp.take(moved, source, axis=0).T.astype(jnp.bfloat16)
    rows = jnp.concatenate([rows, jnp.pad(shift, ((0, 16 - half), (0, tile - atoms)))], axis=0)
    other = across(rows)
    plan = make_plan(atom_owner, block_sizes, place, c_offsets, half, (rows, other))
    table = join(table, (tail, across(tail)), (head, across(head)), False)
    return products(plan, [(rows, other)], table, tuple(range(atoms)), **common)


def solution(mesh):
    placed = (
        P(("groups", "row"), "col", None, None, "layer", None, None),
        P(("groups", "row"), "col", None, None, "layer"),
        P(("groups", "row", "col")),
        P(("groups", "row", "col"), "layer", None, None),
        P("groups", None),
        P(("groups", "row", "col"), None),
        P("groups"),
    )
    return jax.shard_map(
        local,
        mesh=mesh,
        in_specs=placed,
        out_specs=P(("groups", "row", "col"), "layer", None, None),
        check_vma=False,
    )
```
